32 devices in a mesh: tm: 4 (over y, x), space: 8 (over z, core).
Axes of the slice: x: 2, y: 2, z: 4, core: 2. Of those that a mesh axis runs over, the one named last changes fastest.
Arguments:
- anomalies: bfloat16 [16, 128, 32768], P('tm', None, 'space'), may hold values from -51 to 51
- obs_index: int32 [16, 8192], P('tm', 'space'), may hold values from 0 to 4095
- obs_weight: float32 [16, 8192], P('tm', 'space'), may hold values from 0.01 to 0.12
Outputs:
- smoothed: bfloat16 [16, 128, 32768], P('tm', None, 'space')
The draws below stay inside these ranges and needn't reach their ends.
All inputs are finite; a program needn't handle non-finite values.
Results may differ from the reference program's by a relative error of at most 0.0034.
Values sent between devices are 32-bit elements; how exact they have to be, the bound alone decides.
A program may use at most 64 MiB of HBM per device.

```python
import math
import jax
import jax.numpy as jnp
from jax import lax

M = 128
CELLS = 4096
OBS_DEV = 1024
TIMES = 16
NCELLS = 32768
OBS = 8192


def mix_members(noise, key):
    order_keys = jax.random.split(key, 2 * TIMES)
    first_order = jax.vmap(lambda single_key: jax.random.permutation(single_key, M))(order_keys[:TIMES])
    second_order = jax.vmap(lambda single_key: jax.random.permutation(single_key, M))(order_keys[TIMES:])
    reorder = jax.vmap(lambda member_block, member_order: jnp.take(member_block, member_order, axis=0))
    return noise + 0.8 * reorder(noise, first_order) + 0.6 * reorder(noise, second_order)


def draw_anomalies(key, part):
    keys = jax.random.split(jax.random.fold_in(key, 11), 5)
    noise = jnp.clip(jax.random.normal(keys[0], (TIMES, M, NCELLS), jnp.float32), -5.0, 5.0)
    member_scale = jnp.exp(jax.random.uniform(keys[3], (TIMES, M, 1), jnp.float32, math.log(0.3), math.log(3.0)))
    mixed = mix_members(noise, keys[4])
    common = jnp.clip(jax.random.normal(keys[1], (TIMES, 1, NCELLS), jnp.float32), -5.0, 5.0)
    loading = 0.8 * jnp.clip(jax.random.normal(keys[2], (TIMES, M, 1), jnp.float32), -3.0, 3.0)
    return jnp.clip(member_scale * (mixed + loading * common), -51.0, 51.0).astype(jnp.bfloat16)


def draw_obs_weight(key, part):
    local_key = jax.random.fold_in(key, 23)
    tile_block = (jnp.arange(OBS) // OBS_DEV).astype(jnp.float32)
    ramp = 1.0 + 2.0 * tile_block / max(OBS // OBS_DEV - 1, 1)
    base = jnp.exp(jax.random.uniform(local_key, (TIMES, OBS), jnp.float32, math.log(0.01), math.log(0.04)))
    return (base * ramp[None, :]).astype(jnp.float32)


def plant(values, own_key, low, largest):
    longest = values.shape.index(max(values.shape))
    spots = []
    for shift in (0, 1):
        where = [jax.random.randint(jax.random.fold_in(own_key, axis), (), 0, length) for axis, length in enumerate(values.shape)]
        where[longest] = (where[longest] + shift) % values.shape[longest]
        spots.append(tuple(where))
    return values.at[spots[0]].set(low).at[spots[1]].set(largest)


def setup_inputs(seed: int = 0) -> dict:
    streams_of = jax.random.split(jax.random.key(seed), 4)
    anomalies = draw_anomalies(jax.random.fold_in(streams_of[3], 71), 0)
    obs_index = plant(jax.random.randint(streams_of[1], (TIMES, OBS), 0, CELLS), jax.random.fold_in(streams_of[1], 1), 0, CELLS - 1).astype(jnp.int32)
    obs_weight = draw_obs_weight(jax.random.fold_in(streams_of[3], 71), 0)
    return dict(anomalies=anomalies, obs_index=obs_index, obs_weight=obs_weight)


def reference(anomalies, obs_index, obs_weight):
    spread_dof = float(M - 1)
    tile_block = (jnp.arange(OBS) // OBS_DEV).astype(jnp.int32)
    global_index = (obs_index + tile_block[None, :] * CELLS).astype(jnp.int32)
    picked = jnp.take_along_axis(anomalies, jnp.broadcast_to(global_index[:, None, :], (TIMES, M, OBS)), axis=2)
    scaled = (picked.astype(jnp.float32) * obs_weight[:, None, :]).astype(jnp.bfloat16)
    wide = scaled.astype(jnp.float32)
    gram = jnp.einsum('tmo,tno->tmn', wide, wide)
    identity = jnp.eye(M, dtype=jnp.float32)
    weights = spread_dof * jnp.linalg.solve(spread_dof * identity + gram, jnp.broadcast_to(identity, gram.shape))

    def advance(running, weight_now):
        return (jnp.dot(weight_now, running, precision=lax.Precision.HIGHEST), running)
    _, chains = lax.scan(advance, identity, weights, reverse=True)

    def smooth_one(pair):
        chain_now, ensemble = pair
        return jnp.dot(chain_now.T.astype(jnp.bfloat16).astype(jnp.float32), ensemble.astype(jnp.float32), preferred_element_type=jnp.float32).astype(jnp.bfloat16)
    return lax.map(smooth_one, (chains, anomalies))
```

```python
import functools
import math

import jax
import jax.numpy as jnp
from jax import lax
from jax.experimental import pallas as pl
from jax.experimental.pallas import tpu as pltpu
from jax.sharding import PartitionSpec as P

MESH = pl.DeviceIdType.MESH
HIGHEST = lax.Precision.HIGHEST
GROUPS = 4
LARGEST_SCALED = 51.0 * 0.12


def exact_dot(left, right):
    return jnp.dot(left, right, precision=HIGHEST, preferred_element_type=jnp.float32)


def gram_kernel(anomalies_ref, index_ref, weight_ref, gram_ref):
    time = pl.program_id(0)
    members, cells = anomalies_ref.shape[1:]
    obs = index_ref.shape[1]
    span = cells // GROUPS
    shift = span.bit_length() - 1
    chunk = 256 if obs % 256 == 0 else obs
    index = index_ref[pl.ds(time, 1), :]
    weight = weight_ref[pl.ds(time, 1), :]
    low = jnp.bitwise_and(index, span - 1)
    high = lax.shift_right_logical(index, shift)
    stacked = jnp.concatenate(
        [anomalies_ref[0, :, g * span:(g + 1) * span] for g in range(GROUPS)], axis=0
    )
    cell_ids = lax.broadcasted_iota(jnp.int32, (span, chunk), 0)
    total = jnp.zeros((members, members), jnp.float32)
    for start in range(0, obs, chunk):
        part = slice(start, start + chunk)
        selector = (cell_ids == low[:, part]).astype(jnp.float32).astype(jnp.bfloat16)
        picked = jnp.dot(stacked, selector, preferred_element_type=jnp.float32)
        scaled = jnp.zeros((members, chunk), jnp.float32)
        for g in range(GROUPS):
            group_weight = jnp.where(high[:, part] == g, weight[:, part], 0.0)
            scaled = scaled + picked[g * members:(g + 1) * members] * group_weight
        scaled = scaled.astype(jnp.bfloat16)
        total = total + lax.dot_general(
            scaled, scaled, (((1,), (1,)), ((), ())), preferred_element_type=jnp.float32
        )
    gram_ref[0] = total


def inverse_of(matrix, identity, steps, both_ref):
    norm = jnp.max(jnp.sum(jnp.abs(matrix), axis=1, keepdims=True), axis=0, keepdims=True)
    least = 1.0 / norm
    size = matrix.shape[0]
    both_ref[:size] = matrix * least
    both_ref[size:] = identity * least

    def step(_, least):
        alpha = 2.0 / (1.0 + least)
        factor = (2.0 * alpha) * identity - (alpha * alpha) * both_ref[:size]
        both_ref[...] = exact_dot(both_ref[...], factor)
        return 4.0 * least / ((1.0 + least) * (1.0 + least))

    lax.fori_loop(0, steps, step, least)
    return both_ref[size:]


def tree(items):
    while len(items) > 1:
        paired = [exact_dot(a, b) for a, b in zip(items[::2], items[1::2])]
        items = paired + items[len(items) - len(items) % 2:]
    return items[0]


def chain_kernel(space, tm, times, steps, gram_ref, out_ref, landed, matrix, weights, products, both_ref,
                 scatter_send, scatter_recv, share_send, share_recv, spread_send, spread_recv,
                 pass_send, pass_recv, time_send, time_recv, relay_send, relay_recv):
    members = matrix.shape[0]
    me = lax.axis_index("space")
    mine = lax.axis_index("tm")
    rows = times * members // space
    team = space // times
    owned = me // team
    place = me % team
    base = owned * team

    def row_slice(number):
        return pl.ds(pl.multiple_of(number * rows, rows), rows)

    def to(source, target, send, recv, **device):
        return pltpu.make_async_remote_copy(
            src_ref=source, dst_ref=target, send_sem=send, recv_sem=recv,
            device_id=device, device_id_type=MESH,
        )

    barrier = pltpu.get_barrier_semaphore()
    for d in range(1, space):
        pl.semaphore_signal(barrier, inc=1, device_id={"space": (me + d) % space}, device_id_type=MESH)
    for d in range(1, tm):
        pl.semaphore_signal(barrier, inc=1, device_id={"tm": (mine + d) % tm}, device_id_type=MESH)
    pl.semaphore_wait(barrier, space + tm - 2)

    sends = []
    for d in range(1, space):
        peer = (me + d) % space
        copy = to(gram_ref.at[row_slice(peer)], landed.at[d], scatter_send.at[d],
                  scatter_recv.at[d], space=peer)
        copy.start()
        sends.append(copy)
    for copy in sends:
        copy.wait_recv()
    total = gram_ref[row_slice(me), :]
    for d in range(1, space):
        total = total + landed[d]
    matrix[row_slice(place), :] = total
    shares = []
    for d in range(1, team):
        peer = (place + d) % team
        copy = to(matrix.at[row_slice(place)], matrix.at[row_slice(place)], share_send.at[d],
                  share_recv.at[d], space=base + peer)
        copy.start()
        shares.append(copy)
    for d in range(1, team):
        origin = (place + team - d) % team
        to(matrix.at[row_slice(origin)], matrix.at[row_slice(origin)], share_send.at[d],
           share_recv.at[d], space=base + origin).wait_recv()

    identity = (
        lax.broadcasted_iota(jnp.int32, (members, members), 0)
        == lax.broadcasted_iota(jnp.int32, (members, members), 1)
    ).astype(jnp.float32)
    spread = float(members - 1)
    weights[owned] = inverse_of(identity + matrix[...] / spread, identity, steps, both_ref)

    def own_rows(slot):
        return weights.at[slot, row_slice(place)]

    for d in range(1, times):
        copy = to(own_rows(owned), own_rows(owned), spread_send.at[d], spread_recv.at[d],
                  space=((owned + d) % times) * team + place)
        copy.start()
        sends.append(copy)
    for d in range(1, times):
        slot = (owned + times - d) % times
        to(own_rows(slot), own_rows(slot), spread_send.at[d], spread_recv.at[d],
           space=slot * team + place).wait_recv()
        for e in range(1, team):
            copy = to(own_rows(slot), own_rows(slot), pass_send.at[d, e], pass_recv.at[d, e],
                      space=base + (place + e) % team)
            copy.start()
            sends.append(copy)
    for d in range(1, times):
        slot = (owned + times - d) % times
        for e in range(1, team):
            origin = (place + team - e) % team
            there = weights.at[slot, row_slice(origin)]
            to(there, there, pass_send.at[d, e], pass_recv.at[d, e], space=base + origin).wait_recv()

    each = [weights[t] for t in range(times)]
    products[mine] = tree(each)

    def product_rows(slot, number):
        return products.at[slot, row_slice(number)]

    for d in range(1, tm):
        @pl.when(mine >= d)
        def _(d=d):
            to(product_rows(mine, place), product_rows(mine, place), time_send.at[d],
               time_recv.at[d], tm=jnp.maximum(mine - d, 0)).start()

    tails = [identity]
    for t in range(times - 1, 0, -1):
        tails.append(exact_dot(each[t], tails[-1]) if t < times - 1 else each[t])
    tails = tails[::-1]

    for d in range(1, tm):
        @pl.when(mine + d < tm)
        def _(d=d):
            slot = jnp.minimum(mine + d, tm - 1)
            to(product_rows(slot, place), product_rows(slot, place), time_send.at[d],
               time_recv.at[d], tm=slot).wait_recv()
            for e in range(1, team):
                to(product_rows(slot, place), product_rows(slot, place), relay_send.at[d, e],
                   relay_recv.at[d, e], space=base + (place + e) % team).start()
    for d in range(1, tm):
        @pl.when(mine + d < tm)
        def _(d=d):
            slot = jnp.minimum(mine + d, tm - 1)
            for e in range(1, team):
                origin = (place + team - e) % team
                to(product_rows(slot, origin), product_rows(slot, origin), relay_send.at[d, e],
                   relay_recv.at[d, e], space=base + origin).wait_recv()

    later = [jnp.where(slot > mine, products[slot], identity) for slot in range(1, tm)]
    suffix = tree(later) if later else identity
    chains = exact_dot(jnp.concatenate(tails, axis=0), suffix)
    for t in range(times):
        out_ref[t] = chains[t * members:(t + 1) * members].T.astype(out_ref.dtype)

    for copy in sends + shares:
        copy.wait_send()
    for d in range(1, tm):
        @pl.when(mine >= d)
        def _(d=d):
            to(product_rows(mine, place), product_rows(mine, place), time_send.at[d],
               time_recv.at[d], tm=jnp.maximum(mine - d, 0)).wait_send()

        @pl.when(mine + d < tm)
        def _(d=d):
            slot = jnp.minimum(mine + d, tm - 1)
            for e in range(1, team):
                to(product_rows(slot, place), product_rows(slot, place), relay_send.at[d, e],
                   relay_recv.at[d, e], space=base + (place + e) % team).wait_send()


def smooth_kernel(chain_ref, anomalies_ref, out_ref):
    out_ref[0] = jnp.dot(
        chain_ref[0], anomalies_ref[0], preferred_element_type=jnp.float32
    ).astype(out_ref.dtype)


def per_device(space, tm, anomalies, obs_index, obs_weight):
    times, members, cells = anomalies.shape
    obs = obs_index.shape[1]
    whole_vmem = pl.BlockSpec(memory_space=pltpu.VMEM)
    one_time = pl.BlockSpec((1, members, cells), lambda t: (t, 0, 0))
    square = pl.BlockSpec((1, members, members), lambda t: (t, 0, 0))
    gram = pl.pallas_call(
        gram_kernel,
        grid=(times,),
        in_specs=[one_time, whole_vmem, whole_vmem],
        out_specs=square,
        out_shape=jax.ShapeDtypeStruct((times, members, members), jnp.float32),
        compiler_params=pltpu.CompilerParams(vmem_limit_bytes=40 * 2**20),
    )(anomalies, obs_index, obs_weight)

    bound = 1.0 + members * obs * space * LARGEST_SCALED**2 / (members - 1)
    steps = math.ceil(math.log(bound / 4.0, 4)) + 4
    rows = times * members // space
    team = space // times
    dma = pltpu.SemaphoreType.DMA
    chains = pl.pallas_call(
        functools.partial(chain_kernel, space, tm, times, steps),
        in_specs=[whole_vmem],
        out_specs=whole_vmem,
        out_shape=jax.ShapeDtypeStruct((times, members, members), jnp.bfloat16),
        scratch_shapes=[
            pltpu.VMEM((space, rows, members), jnp.float32),
            pltpu.VMEM((members, members), jnp.float32),
            pltpu.VMEM((times, members, members), jnp.float32),
            pltpu.VMEM((tm, members, members), jnp.float32),
            pltpu.VMEM((2 * members, members), jnp.float32),
            dma((space,)), dma((space,)), dma((team,)), dma((team,)), dma((times,)), dma((times,)),
            dma((times, team)), dma((times, team)), dma((tm,)), dma((tm,)),
            dma((tm, team)), dma((tm, team)),
        ],
        compiler_params=pltpu.CompilerParams(
            collective_id=0, has_side_effects=True, vmem_limit_bytes=40 * 2**20
        ),
    )(gram.reshape(times * members, members))

    return pl.pallas_call(
        smooth_kernel,
        grid=(times,),
        in_specs=[square, one_time],
        out_specs=one_time,
        out_shape=jax.ShapeDtypeStruct(anomalies.shape, anomalies.dtype),
        compiler_params=pltpu.CompilerParams(vmem_limit_bytes=40 * 2**20),
    )(chains, anomalies)


def solution(mesh):
    return jax.shard_map(
        functools.partial(per_device, mesh.shape["space"], mesh.shape["tm"]),
        mesh=mesh,
        in_specs=(P("tm", None, "space"), P("tm", "space"), P("tm", "space")),
        out_specs=P("tm", None, "space"),
        check_vma=False,
    )
```

```python
import functools
import math

import jax
import jax.numpy as jnp
from jax import lax
from jax.experimental import pallas as pl
from jax.experimental.pallas import tpu as pltpu
from jax.sharding import PartitionSpec as P

MESH = pl.DeviceIdType.MESH
GROUPS = 4
LARGEST_SCALED = 51.0 * 0.12


def split(value):
    high = value.astype(jnp.bfloat16)
    rest = value - high.astype(jnp.float32)
    middle = rest.astype(jnp.bfloat16)
    low = (rest - middle.astype(jnp.float32)).astype(jnp.bfloat16)
    return high, middle, low


def exact_dot(left, right):
    width = right.shape[1]
    left_high, left_middle, left_low = split(left)
    right_high, right_middle, right_low = split(right)
    main_left = jnp.concatenate([left_high, left_middle], axis=1)
    main_row = jnp.concatenate([right_high, right_middle], axis=1)
    main_right = jnp.concatenate([main_row, main_row], axis=0)
    rest_left = jnp.concatenate([left_high, left_low], axis=1)
    rest_right = jnp.concatenate([right_low, right_high], axis=0)
    main = jnp.dot(main_left, main_right, preferred_element_type=jnp.float32)
    rest = jnp.dot(rest_left, rest_right, preferred_element_type=jnp.float32)
    return main[:, :width] + (main[:, width:] + rest)


def gram_kernel(anomalies_ref, index_ref, weight_ref, gram_ref):
    time = pl.program_id(0)
    members, cells = anomalies_ref.shape[1:]
    obs = index_ref.shape[1]
    span = cells // GROUPS
    shift = span.bit_length() - 1
    chunk = 256 if obs % 256 == 0 else obs
    index = index_ref[pl.ds(time, 1), :]
    weight = weight_ref[pl.ds(time, 1), :]
    low = jnp.bitwise_and(index, span - 1)
    high = lax.shift_right_logical(index, shift)
    stacked = jnp.concatenate(
        [anomalies_ref[0, :, g * span:(g + 1) * span] for g in range(GROUPS)], axis=0
    )
    cell_ids = lax.broadcasted_iota(jnp.int32, (span, chunk), 0)
    total = jnp.zeros((members, members), jnp.float32)
    for start in range(0, obs, chunk):
        part = slice(start, start + chunk)
        selector = (cell_ids == low[:, part]).astype(jnp.float32).astype(jnp.bfloat16)
        picked = jnp.dot(stacked, selector, preferred_element_type=jnp.float32)
        scaled = jnp.zeros((members, chunk), jnp.float32)
        for g in range(GROUPS):
            group_weight = jnp.where(high[:, part] == g, weight[:, part], 0.0)
            scaled = scaled + picked[g * members:(g + 1) * members] * group_weight
        scaled = scaled.astype(jnp.bfloat16)
        total = total + lax.dot_general(
            scaled, scaled, (((1,), (1,)), ((), ())), preferred_element_type=jnp.float32
        )
    gram_ref[0] = total


def inverse_of(matrix, identity, steps, both_ref):
    norm = jnp.max(jnp.sum(jnp.abs(matrix), axis=1, keepdims=True), axis=0, keepdims=True)
    least = 1.0 / norm
    size = matrix.shape[0]
    both_ref[:size] = matrix * least
    both_ref[size:] = identity * least

    def step(_, least):
        alpha = 2.0 / (1.0 + least)
        factor = (2.0 * alpha) * identity - (alpha * alpha) * both_ref[:size]
        both_ref[...] = exact_dot(both_ref[...], factor)
        return 4.0 * least / ((1.0 + least) * (1.0 + least))

    lax.fori_loop(0, steps, step, least)
    return both_ref[size:]


def tree(items):
    while len(items) > 1:
        paired = [exact_dot(a, b) for a, b in zip(items[::2], items[1::2])]
        items = paired + items[len(items) - len(items) % 2:]
    return items[0]


def chain_kernel(space, tm, times, steps, gram_ref, out_ref, landed, matrix, weights, products, both_ref,
                 scatter_send, scatter_recv, share_send, share_recv, spread_send, spread_recv,
                 pass_send, pass_recv, time_send, time_recv, relay_send, relay_recv):
    members = matrix.shape[0]
    me = lax.axis_index("space")
    mine = lax.axis_index("tm")
    rows = times * members // space
    team = space // times
    owned = me // team
    place = me % team
    base = owned * team

    def row_slice(number):
        return pl.ds(pl.multiple_of(number * rows, rows), rows)

    def to(source, target, send, recv, **device):
        return pltpu.make_async_remote_copy(
            src_ref=source, dst_ref=target, send_sem=send, recv_sem=recv,
            device_id=device, device_id_type=MESH,
        )

    barrier = pltpu.get_barrier_semaphore()
    for d in range(1, space):
        pl.semaphore_signal(barrier, inc=1, device_id={"space": (me + d) % space}, device_id_type=MESH)
    for d in range(1, tm):
        pl.semaphore_signal(barrier, inc=1, device_id={"tm": (mine + d) % tm}, device_id_type=MESH)
    pl.semaphore_wait(barrier, space + tm - 2)

    sends = []
    for d in range(1, space):
        peer = (me + d) % space
        copy = to(gram_ref.at[row_slice(peer)], landed.at[d], scatter_send.at[d],
                  scatter_recv.at[d], space=peer)
        copy.start()
        sends.append(copy)
    for copy in sends:
        copy.wait_recv()
    total = gram_ref[row_slice(me), :]
    for d in range(1, space):
        total = total + landed[d]
    matrix[row_slice(place), :] = total
    shares = []
    for d in range(1, team):
        peer = (place + d) % team
        copy = to(matrix.at[row_slice(place)], matrix.at[row_slice(place)], share_send.at[d],
                  share_recv.at[d], space=base + peer)
        copy.start()
        shares.append(copy)
    for d in range(1, team):
        origin = (place + team - d) % team
        to(matrix.at[row_slice(origin)], matrix.at[row_slice(origin)], share_send.at[d],
           share_recv.at[d], space=base + origin).wait_recv()

    identity = (
        lax.broadcasted_iota(jnp.int32, (members, members), 0)
        == lax.broadcasted_iota(jnp.int32, (members, members), 1)
    ).astype(jnp.float32)
    spread = float(members - 1)
    weights[owned] = inverse_of(identity + matrix[...] / spread, identity, steps, both_ref)

    def own_rows(slot):
        return weights.at[slot, row_slice(place)]

    for d in range(1, times):
        copy = to(own_rows(owned), own_rows(owned), spread_send.at[d], spread_recv.at[d],
                  space=((owned + d) % times) * team + place)
        copy.start()
        sends.append(copy)
    for d in range(1, times):
        slot = (owned + times - d) % times
        to(own_rows(slot), own_rows(slot), spread_send.at[d], spread_recv.at[d],
           space=slot * team + place).wait_recv()
        for e in range(1, team):
            copy = to(own_rows(slot), own_rows(slot), pass_send.at[d, e], pass_recv.at[d, e],
                      space=base + (place + e) % team)
            copy.start()
            sends.append(copy)
    for d in range(1, times):
        slot = (owned + times - d) % times
        for e in range(1, team):
            origin = (place + team - e) % team
            there = weights.at[slot, row_slice(origin)]
            to(there, there, pass_send.at[d, e], pass_recv.at[d, e], space=base + origin).wait_recv()

    each = [weights[t] for t in range(times)]
    products[mine] = tree(each)

    def product_rows(slot, number):
        return products.at[slot, row_slice(number)]

    for d in range(1, tm):
        @pl.when(mine >= d)
        def _(d=d):
            to(product_rows(mine, place), product_rows(mine, place), time_send.at[d],
               time_recv.at[d], tm=jnp.maximum(mine - d, 0)).start()

    tails = [identity]
    for t in range(times - 1, 0, -1):
        tails.append(exact_dot(each[t], tails[-1]) if t < times - 1 else each[t])
    tails = tails[::-1]

    for d in range(1, tm):
        @pl.when(mine + d < tm)
        def _(d=d):
            slot = jnp.minimum(mine + d, tm - 1)
            to(product_rows(slot, place), product_rows(slot, place), time_send.at[d],
               time_recv.at[d], tm=slot).wait_recv()
            for e in range(1, team):
                to(product_rows(slot, place), product_rows(slot, place), relay_send.at[d, e],
                   relay_recv.at[d, e], space=base + (place + e) % team).start()
    for d in range(1, tm):
        @pl.when(mine + d < tm)
        def _(d=d):
            slot = jnp.minimum(mine + d, tm - 1)
            for e in range(1, team):
                origin = (place + team - e) % team
                to(product_rows(slot, origin), product_rows(slot, origin), relay_send.at[d, e],
                   relay_recv.at[d, e], space=base + origin).wait_recv()

    later = [jnp.where(slot > mine, products[slot], identity) for slot in range(1, tm)]
    suffix = tree(later) if later else identity
    chains = exact_dot(jnp.concatenate(tails, axis=0), suffix)
    for t in range(times):
        out_ref[t] = chains[t * members:(t + 1) * members].T.astype(out_ref.dtype)

    for copy in sends + shares:
        copy.wait_send()
    for d in range(1, tm):
        @pl.when(mine >= d)
        def _(d=d):
            to(product_rows(mine, place), product_rows(mine, place), time_send.at[d],
               time_recv.at[d], tm=jnp.maximum(mine - d, 0)).wait_send()

        @pl.when(mine + d < tm)
        def _(d=d):
            slot = jnp.minimum(mine + d, tm - 1)
            for e in range(1, team):
                to(product_rows(slot, place), product_rows(slot, place), relay_send.at[d, e],
                   relay_recv.at[d, e], space=base + (place + e) % team).wait_send()


def smooth_kernel(chain_ref, anomalies_ref, out_ref):
    out_ref[0] = jnp.dot(
        chain_ref[0], anomalies_ref[0], preferred_element_type=jnp.float32
    ).astype(out_ref.dtype)


def per_device(space, tm, anomalies, obs_index, obs_weight):
    times, members, cells = anomalies.shape
    obs = obs_index.shape[1]
    whole_vmem = pl.BlockSpec(memory_space=pltpu.VMEM)
    one_time = pl.BlockSpec((1, members, cells), lambda t: (t, 0, 0))
    square = pl.BlockSpec((1, members, members), lambda t: (t, 0, 0))
    gram = pl.pallas_call(
        gram_kernel,
        grid=(times,),
        in_specs=[one_time, whole_vmem, whole_vmem],
        out_specs=square,
        out_shape=jax.ShapeDtypeStruct((times, members, members), jnp.float32),
        compiler_params=pltpu.CompilerParams(vmem_limit_bytes=40 * 2**20),
    )(anomalies, obs_index, obs_weight)

    bound = 1.0 + members * obs * space * LARGEST_SCALED**2 / (members - 1)
    steps = math.ceil(math.log(bound / 4.0, 4)) + 3
    rows = times * members // space
    team = space // times
    dma = pltpu.SemaphoreType.DMA
    chains = pl.pallas_call(
        functools.partial(chain_kernel, space, tm, times, steps),
        in_specs=[whole_vmem],
        out_specs=whole_vmem,
        out_shape=jax.ShapeDtypeStruct((times, members, members), jnp.bfloat16),
        scratch_shapes=[
            pltpu.VMEM((space, rows, members), jnp.float32),
            pltpu.VMEM((members, members), jnp.float32),
            pltpu.VMEM((times, members, members), jnp.float32),
            pltpu.VMEM((tm, members, members), jnp.float32),
            pltpu.VMEM((2 * members, members), jnp.float32),
            dma((space,)), dma((space,)), dma((team,)), dma((team,)), dma((times,)), dma((times,)),
            dma((times, team)), dma((times, team)), dma((tm,)), dma((tm,)),
            dma((tm, team)), dma((tm, team)),
        ],
        compiler_params=pltpu.CompilerParams(
            collective_id=0, has_side_effects=True, vmem_limit_bytes=40 * 2**20
        ),
    )(gram.reshape(times * members, members))

    return pl.pallas_call(
        smooth_kernel,
        grid=(times,),
        in_specs=[square, one_time],
        out_specs=one_time,
        out_shape=jax.ShapeDtypeStruct(anomalies.shape, anomalies.dtype),
        compiler_params=pltpu.CompilerParams(vmem_limit_bytes=40 * 2**20),
    )(chains, anomalies)


def solution(mesh):
    return jax.shard_map(
        functools.partial(per_device, mesh.shape["space"], mesh.shape["tm"]),
        mesh=mesh,
        in_specs=(P("tm", None, "space"), P("tm", "space"), P("tm", "space")),
        out_specs=P("tm", None, "space"),
        check_vma=False,
    )
```

```python
import functools
import math

import jax
import jax.numpy as jnp
from jax import lax
from jax.experimental import pallas as pl
from jax.experimental.pallas import tpu as pltpu
from jax.sharding import PartitionSpec as P

MESH = pl.DeviceIdType.MESH
GROUPS = 4
LARGEST_SCALED = 51.0 * 0.12


def split(value):
    high = value.astype(jnp.bfloat16)
    rest = value - high.astype(jnp.float32)
    middle = rest.astype(jnp.bfloat16)
    low = (rest - middle.astype(jnp.float32)).astype(jnp.bfloat16)
    return high, middle, low


def exact_dot(left, right):
    width = right.shape[1]
    left_high, left_middle, left_low = split(left)
    right_high, right_middle, right_low = split(right)
    main_left = jnp.concatenate([left_high, left_middle], axis=1)
    main_row = jnp.concatenate([right_high, right_middle], axis=1)
    main_right = jnp.concatenate([main_row, main_row], axis=0)
    rest_left = jnp.concatenate([left_high, left_low], axis=1)
    rest_right = jnp.concatenate([right_low, right_high], axis=0)
    main = jnp.dot(main_left, main_right, preferred_element_type=jnp.float32)
    rest = jnp.dot(rest_left, rest_right, preferred_element_type=jnp.float32)
    return main[:, :width] + (main[:, width:] + rest)


def gram_of(cells_at, index, weight):
    members, cells = cells_at.shape
    obs = index.shape[1]
    span = cells // GROUPS
    shift = span.bit_length() - 1
    chunk = 256 if obs % 256 == 0 else obs
    low = jnp.bitwise_and(index, span - 1)
    high = lax.shift_right_logical(index, shift)
    stacked = jnp.concatenate(
        [cells_at[:, g * span:(g + 1) * span] for g in range(GROUPS)], axis=0
    )
    cell_ids = lax.broadcasted_iota(jnp.int32, (span, chunk), 0)
    total = jnp.zeros((members, members), jnp.float32)
    for start in range(0, obs, chunk):
        part = slice(start, start + chunk)
        selector = (cell_ids == low[:, part]).astype(jnp.float32).astype(jnp.bfloat16)
        picked = jnp.dot(stacked, selector, preferred_element_type=jnp.float32)
        scaled = jnp.zeros((members, chunk), jnp.float32)
        for g in range(GROUPS):
            group_weight = jnp.where(high[:, part] == g, weight[:, part], 0.0)
            scaled = scaled + picked[g * members:(g + 1) * members] * group_weight
        scaled = scaled.astype(jnp.bfloat16)
        total = total + lax.dot_general(
            scaled, scaled, (((1,), (1,)), ((), ())), preferred_element_type=jnp.float32
        )
    return total


def inverse_of(matrix, identity, steps, both_ref):
    norm = jnp.max(jnp.sum(jnp.abs(matrix), axis=1, keepdims=True), axis=0, keepdims=True)
    least = 1.0 / norm
    size = matrix.shape[0]
    both_ref[:size] = matrix * least
    both_ref[size:] = identity * least

    def step(_, least):
        alpha = 2.0 / (1.0 + least)
        factor = (2.0 * alpha) * identity - (alpha * alpha) * both_ref[:size]
        both_ref[...] = exact_dot(both_ref[...], factor)
        return 4.0 * least / ((1.0 + least) * (1.0 + least))

    lax.fori_loop(0, steps, step, least)
    return both_ref[size:]


def tree(items):
    while len(items) > 1:
        paired = [exact_dot(a, b) for a, b in zip(items[::2], items[1::2])]
        items = paired + items[len(items) - len(items) % 2:]
    return items[0]


def chain_kernel(space, tm, times, steps, anomalies_ref, index_ref, weight_ref, out_ref,
                 cells, index, weight, gram, landed, partner, matrix, weights, products, both_ref,
                 load_sem, index_sem, weight_sem,
                 scatter_send, scatter_recv, partner_send, partner_recv, share_send, share_recv,
                 spread_send, spread_recv, pass_send, pass_recv, time_send, time_recv,
                 relay_send, relay_recv):
    members = matrix.shape[0]
    me = lax.axis_index("space")
    mine = lax.axis_index("tm")
    rows = times * members // space
    team = space // times
    owned = me // team
    place = me % team
    base = owned * team

    def row_slice(number):
        return pl.ds(pl.multiple_of(number * rows, rows), rows)

    def to(source, target, send, recv, **device):
        return pltpu.make_async_remote_copy(
            src_ref=source, dst_ref=target, send_sem=send, recv_sem=recv,
            device_id=device, device_id_type=MESH,
        )

    order = [(owned + 1 + i) % times for i in range(times)]
    index_load = pltpu.make_async_copy(index_ref, index, index_sem)
    weight_load = pltpu.make_async_copy(weight_ref, weight, weight_sem)
    loads = [
        pltpu.make_async_copy(anomalies_ref.at[slot], cells.at[i], load_sem.at[i])
        for i, slot in enumerate(order)
    ]
    index_load.start()
    loads[0].start()
    weight_load.start()
    for load in loads[1:]:
        load.start()

    barrier = pltpu.get_barrier_semaphore()
    for d in range(1, space):
        pl.semaphore_signal(barrier, inc=1, device_id={"space": (me + d) % space}, device_id_type=MESH)
    for d in range(1, tm):
        pl.semaphore_signal(barrier, inc=1, device_id={"tm": (mine + d) % tm}, device_id_type=MESH)
    index_load.wait()
    weight_load.wait()

    sends = []
    for i, slot in enumerate(order):
        loads[i].wait()
        gram[slot] = gram_of(cells.at[i], index[pl.ds(slot, 1), :], weight[pl.ds(slot, 1), :])
        if i == 0:
            pl.semaphore_wait(barrier, space + tm - 2)
        if i < times - 1:
            for e in range(team):
                peer = (place + e) % team
                copy = to(gram.at[slot, row_slice(peer)], landed.at[i, e], scatter_send.at[i, e],
                          scatter_recv.at[i, e], space=slot * team + peer)
                copy.start()
                sends.append(copy)
    partners = []
    for e in range(1, team):
        copy = to(gram.at[owned], partner.at[e], partner_send.at[e], partner_recv.at[e],
                  space=base + (place + e) % team)
        copy.start()
        partners.append(copy)
    for copy in sends:
        copy.wait_recv()
    matrix[row_slice(place), :] = jnp.sum(
        landed[...].reshape((times - 1) * team, rows, members), axis=0
    )
    shares = []
    for e in range(1, team):
        copy = to(matrix.at[row_slice(place)], matrix.at[row_slice(place)], share_send.at[e],
                  share_recv.at[e], space=base + (place + e) % team)
        copy.start()
        shares.append(copy)
    total = gram[owned]
    for copy in partners:
        copy.wait_recv()
    for e in range(1, team):
        total = total + partner[e]
    for e in range(1, team):
        origin = (place + team - e) % team
        to(matrix.at[row_slice(origin)], matrix.at[row_slice(origin)], share_send.at[e],
           share_recv.at[e], space=base + origin).wait_recv()
    total = total + matrix[...]

    identity = (
        lax.broadcasted_iota(jnp.int32, (members, members), 0)
        == lax.broadcasted_iota(jnp.int32, (members, members), 1)
    ).astype(jnp.float32)
    spread = float(members - 1)
    weights[owned] = inverse_of(identity + total / spread, identity, steps, both_ref)

    def own_rows(slot):
        return weights.at[slot, row_slice(place)]

    for d in range(1, times):
        copy = to(own_rows(owned), own_rows(owned), spread_send.at[d], spread_recv.at[d],
                  space=((owned + d) % times) * team + place)
        copy.start()
        sends.append(copy)
    for d in range(1, times):
        slot = (owned + times - d) % times
        to(own_rows(slot), own_rows(slot), spread_send.at[d], spread_recv.at[d],
           space=slot * team + place).wait_recv()
        for e in range(1, team):
            copy = to(own_rows(slot), own_rows(slot), pass_send.at[d, e], pass_recv.at[d, e],
                      space=base + (place + e) % team)
            copy.start()
            sends.append(copy)
    for d in range(1, times):
        slot = (owned + times - d) % times
        for e in range(1, team):
            origin = (place + team - e) % team
            there = weights.at[slot, row_slice(origin)]
            to(there, there, pass_send.at[d, e], pass_recv.at[d, e], space=base + origin).wait_recv()

    each = [weights[t] for t in range(times)]
    products[mine] = tree(each)

    def product_rows(slot, number):
        return products.at[slot, row_slice(number)]

    for d in range(1, tm):
        @pl.when(mine >= d)
        def _(d=d):
            to(product_rows(mine, place), product_rows(mine, place), time_send.at[d],
               time_recv.at[d], tm=jnp.maximum(mine - d, 0)).start()

    tails = [identity]
    for t in range(times - 1, 0, -1):
        tails.append(exact_dot(each[t], tails[-1]) if t < times - 1 else each[t])
    tails = tails[::-1]

    for d in range(1, tm):
        @pl.when(mine + d < tm)
        def _(d=d):
            slot = jnp.minimum(mine + d, tm - 1)
            to(product_rows(slot, place), product_rows(slot, place), time_send.at[d],
               time_recv.at[d], tm=slot).wait_recv()
            for e in range(1, team):
                to(product_rows(slot, place), product_rows(slot, place), relay_send.at[d, e],
                   relay_recv.at[d, e], space=base + (place + e) % team).start()
    for d in range(1, tm):
        @pl.when(mine + d < tm)
        def _(d=d):
            slot = jnp.minimum(mine + d, tm - 1)
            for e in range(1, team):
                origin = (place + team - e) % team
                to(product_rows(slot, origin), product_rows(slot, origin), relay_send.at[d, e],
                   relay_recv.at[d, e], space=base + origin).wait_recv()

    later = [jnp.where(slot > mine, products[slot], identity) for slot in range(1, tm)]
    suffix = tree(later) if later else identity
    chains = exact_dot(jnp.concatenate(tails, axis=0), suffix)
    for t in range(times):
        out_ref[t] = chains[t * members:(t + 1) * members].T.astype(out_ref.dtype)

    for copy in sends + shares + partners:
        copy.wait_send()
    for d in range(1, tm):
        @pl.when(mine >= d)
        def _(d=d):
            to(product_rows(mine, place), product_rows(mine, place), time_send.at[d],
               time_recv.at[d], tm=jnp.maximum(mine - d, 0)).wait_send()

        @pl.when(mine + d < tm)
        def _(d=d):
            slot = jnp.minimum(mine + d, tm - 1)
            for e in range(1, team):
                to(product_rows(slot, place), product_rows(slot, place), relay_send.at[d, e],
                   relay_recv.at[d, e], space=base + (place + e) % team).wait_send()


def smooth_kernel(chain_ref, anomalies_ref, out_ref):
    out_ref[0] = jnp.dot(
        chain_ref[0], anomalies_ref[0], preferred_element_type=jnp.float32
    ).astype(out_ref.dtype)


def per_device(space, tm, anomalies, obs_index, obs_weight):
    times, members, cells = anomalies.shape
    obs = obs_index.shape[1]
    whole_vmem = pl.BlockSpec(memory_space=pltpu.VMEM)
    one_time = pl.BlockSpec((1, members, cells), lambda t: (t, 0, 0))
    square = pl.BlockSpec((1, members, members), lambda t: (t, 0, 0))
    bound = 1.0 + members * obs * space * LARGEST_SCALED**2 / (members - 1)
    steps = math.ceil(math.log(bound / 4.0, 4)) + 3
    rows = times * members // space
    team = space // times
    dma = pltpu.SemaphoreType.DMA
    in_hbm = pl.BlockSpec(memory_space=pltpu.HBM)
    wide = jnp.float32
    square_wide = (members, members)
    chains = pl.pallas_call(
        functools.partial(chain_kernel, space, tm, times, steps),
        in_specs=[in_hbm] * 3,
        out_specs=whole_vmem,
        out_shape=jax.ShapeDtypeStruct((times, members, members), jnp.bfloat16),
        scratch_shapes=[
            pltpu.VMEM(anomalies.shape, anomalies.dtype),
            pltpu.VMEM(obs_index.shape, obs_index.dtype),
            pltpu.VMEM(obs_weight.shape, obs_weight.dtype),
            pltpu.VMEM((times, *square_wide), wide),
            pltpu.VMEM((times - 1, team, rows, members), wide),
            pltpu.VMEM((team, *square_wide), wide),
            pltpu.VMEM(square_wide, wide),
            pltpu.VMEM((times, *square_wide), wide),
            pltpu.VMEM((tm, *square_wide), wide),
            pltpu.VMEM((2 * members, members), wide),
            dma((times,)), dma, dma,
            dma((times, team)), dma((times, team)), dma((team,)), dma((team,)),
            dma((team,)), dma((team,)), dma((times,)), dma((times,)),
            dma((times, team)), dma((times, team)), dma((tm,)), dma((tm,)),
            dma((tm, team)), dma((tm, team)),
        ],
        compiler_params=pltpu.CompilerParams(
            collective_id=0, has_side_effects=True, vmem_limit_bytes=63 * 2**20
        ),
    )(anomalies, obs_index, obs_weight)

    return pl.pallas_call(
        smooth_kernel,
        grid=(times,),
        in_specs=[square, one_time],
        out_specs=one_time,
        out_shape=jax.ShapeDtypeStruct(anomalies.shape, anomalies.dtype),
        compiler_params=pltpu.CompilerParams(vmem_limit_bytes=40 * 2**20),
    )(chains, anomalies)


def solution(mesh):
    return jax.shard_map(
        functools.partial(per_device, mesh.shape["space"], mesh.shape["tm"]),
        mesh=mesh,
        in_specs=(P("tm", None, "space"), P("tm", "space"), P("tm", "space")),
        out_specs=P("tm", None, "space"),
        check_vma=False,
    )
```

```python
import functools
import math

import jax
import jax.numpy as jnp
from jax import lax
from jax.experimental import pallas as pl
from jax.experimental.pallas import tpu as pltpu
from jax.sharding import PartitionSpec as P

MESH = pl.DeviceIdType.MESH
GROUPS = 4
LARGEST_SCALED = 51.0 * 0.12


def split(value):
    high = value.astype(jnp.bfloat16)
    rest = value - high.astype(jnp.float32)
    middle = rest.astype(jnp.bfloat16)
    low = (rest - middle.astype(jnp.float32)).astype(jnp.bfloat16)
    return high, middle, low


def exact_dot(left, right):
    width = right.shape[1]
    left_high, left_middle, left_low = split(left)
    right_high, right_middle, right_low = split(right)
    main_left = jnp.concatenate([left_high, left_middle], axis=1)
    main_row = jnp.concatenate([right_high, right_middle], axis=1)
    main_right = jnp.concatenate([main_row, main_row], axis=0)
    rest_left = jnp.concatenate([left_high, left_low], axis=1)
    rest_right = jnp.concatenate([right_low, right_high], axis=0)
    main = jnp.dot(main_left, main_right, preferred_element_type=jnp.float32)
    rest = jnp.dot(rest_left, rest_right, preferred_element_type=jnp.float32)
    return main[:, :width] + (main[:, width:] + rest)


def gram_of(cells_at, index, weight):
    members, cells = cells_at.shape
    obs = index.shape[1]
    span = cells // GROUPS
    shift = span.bit_length() - 1
    chunk = 256 if obs % 256 == 0 else obs
    low = jnp.bitwise_and(index, span - 1)
    high = lax.shift_right_logical(index, shift)
    stacked = jnp.concatenate(
        [cells_at[:, g * span:(g + 1) * span] for g in range(GROUPS)], axis=0
    )
    cell_ids = lax.broadcasted_iota(jnp.int32, (span, chunk), 0)
    total = jnp.zeros((members, members), jnp.float32)
    for start in range(0, obs, chunk):
        part = slice(start, start + chunk)
        selector = (cell_ids == low[:, part]).astype(jnp.float32).astype(jnp.bfloat16)
        picked = jnp.dot(stacked, selector, preferred_element_type=jnp.float32)
        scaled = jnp.zeros((members, chunk), jnp.float32)
        for g in range(GROUPS):
            group_weight = jnp.where(high[:, part] == g, weight[:, part], 0.0)
            scaled = scaled + picked[g * members:(g + 1) * members] * group_weight
        scaled = scaled.astype(jnp.bfloat16)
        total = total + lax.dot_general(
            scaled, scaled, (((1,), (1,)), ((), ())), preferred_element_type=jnp.float32
        )
    return total


def inverse_of(matrix, identity, steps, both_ref):
    norm = jnp.max(jnp.sum(jnp.abs(matrix), axis=1, keepdims=True), axis=0, keepdims=True)
    least = 1.0 / norm
    size = matrix.shape[0]
    both_ref[:size] = matrix * least
    both_ref[size:] = identity * least

    def step(_, least):
        alpha = 2.0 / (1.0 + least)
        factor = (2.0 * alpha) * identity - (alpha * alpha) * both_ref[:size]
        both_ref[...] = exact_dot(both_ref[...], factor)
        return 4.0 * least / ((1.0 + least) * (1.0 + least))

    lax.fori_loop(0, steps, step, least)
    return both_ref[size:]


def tree(items):
    while len(items) > 1:
        paired = [exact_dot(a, b) for a, b in zip(items[::2], items[1::2])]
        items = paired + items[len(items) - len(items) % 2:]
    return items[0]


def chain_kernel(space, tm, times, steps, anomalies_ref, index_ref, weight_ref, out_ref,
                 cells, index, weight, gram, landed, partner, matrix, weights, products, both_ref, chains_ref,
                 load_sem, index_sem, weight_sem,
                 scatter_send, scatter_recv, partner_send, partner_recv, share_send, share_recv,
                 spread_send, spread_recv, pass_send, pass_recv, time_send, time_recv,
                 relay_send, relay_recv):
    members = matrix.shape[0]
    me = lax.axis_index("space")
    mine = lax.axis_index("tm")
    rows = times * members // space
    team = space // times
    owned = me // team
    place = me % team
    base = owned * team

    def row_slice(number):
        return pl.ds(pl.multiple_of(number * rows, rows), rows)

    def to(source, target, send, recv, **device):
        return pltpu.make_async_remote_copy(
            src_ref=source, dst_ref=target, send_sem=send, recv_sem=recv,
            device_id=device, device_id_type=MESH,
        )

    order = [(owned + 1 + i) % times for i in range(times)]
    index_load = pltpu.make_async_copy(index_ref, index, index_sem)
    weight_load = pltpu.make_async_copy(weight_ref, weight, weight_sem)
    loads = [
        pltpu.make_async_copy(anomalies_ref.at[slot], cells.at[i], load_sem.at[i])
        for i, slot in enumerate(order)
    ]
    index_load.start()
    loads[0].start()
    weight_load.start()
    for load in loads[1:]:
        load.start()

    barrier = pltpu.get_barrier_semaphore()
    for d in range(1, space):
        pl.semaphore_signal(barrier, inc=1, device_id={"space": (me + d) % space}, device_id_type=MESH)
    for d in range(1, tm):
        pl.semaphore_signal(barrier, inc=1, device_id={"tm": (mine + d) % tm}, device_id_type=MESH)
    index_load.wait()
    weight_load.wait()

    sends = []
    for i, slot in enumerate(order):
        loads[i].wait()
        gram[slot] = gram_of(cells.at[i], index[pl.ds(slot, 1), :], weight[pl.ds(slot, 1), :])
        if i == 0:
            pl.semaphore_wait(barrier, space + tm - 2)
        if i < times - 1:
            for e in range(team):
                peer = (place + e) % team
                copy = to(gram.at[slot, row_slice(peer)], landed.at[i, e], scatter_send.at[i, e],
                          scatter_recv.at[i, e], space=slot * team + peer)
                copy.start()
                sends.append(copy)
    partners = []
    for e in range(1, team):
        copy = to(gram.at[owned], partner.at[e], partner_send.at[e], partner_recv.at[e],
                  space=base + (place + e) % team)
        copy.start()
        partners.append(copy)
    for copy in sends:
        copy.wait_recv()
    matrix[row_slice(place), :] = jnp.sum(
        landed[...].reshape((times - 1) * team, rows, members), axis=0
    )
    shares = []
    for e in range(1, team):
        copy = to(matrix.at[row_slice(place)], matrix.at[row_slice(place)], share_send.at[e],
                  share_recv.at[e], space=base + (place + e) % team)
        copy.start()
        shares.append(copy)
    total = gram[owned]
    for copy in partners:
        copy.wait_recv()
    for e in range(1, team):
        total = total + partner[e]
    for e in range(1, team):
        origin = (place + team - e) % team
        to(matrix.at[row_slice(origin)], matrix.at[row_slice(origin)], share_send.at[e],
           share_recv.at[e], space=base + origin).wait_recv()
    total = total + matrix[...]

    identity = (
        lax.broadcasted_iota(jnp.int32, (members, members), 0)
        == lax.broadcasted_iota(jnp.int32, (members, members), 1)
    ).astype(jnp.float32)
    spread = float(members - 1)
    weights[owned] = inverse_of(identity + total / spread, identity, steps, both_ref)

    def own_rows(slot):
        return weights.at[slot, row_slice(place)]

    for d in range(1, times):
        copy = to(own_rows(owned), own_rows(owned), spread_send.at[d], spread_recv.at[d],
                  space=((owned + d) % times) * team + place)
        copy.start()
        sends.append(copy)
    for d in range(1, times):
        slot = (owned + times - d) % times
        to(own_rows(slot), own_rows(slot), spread_send.at[d], spread_recv.at[d],
           space=slot * team + place).wait_recv()
        for e in range(1, team):
            copy = to(own_rows(slot), own_rows(slot), pass_send.at[d, e], pass_recv.at[d, e],
                      space=base + (place + e) % team)
            copy.start()
            sends.append(copy)
    for d in range(1, times):
        slot = (owned + times - d) % times
        for e in range(1, team):
            origin = (place + team - e) % team
            there = weights.at[slot, row_slice(origin)]
            to(there, there, pass_send.at[d, e], pass_recv.at[d, e], space=base + origin).wait_recv()

    each = [weights[t] for t in range(times)]
    products[mine] = tree(each)

    def product_rows(slot, number):
        return products.at[slot, row_slice(number)]

    for d in range(1, tm):
        @pl.when(mine >= d)
        def _(d=d):
            to(product_rows(mine, place), product_rows(mine, place), time_send.at[d],
               time_recv.at[d], tm=jnp.maximum(mine - d, 0)).start()

    tails = [identity]
    for t in range(times - 1, 0, -1):
        tails.append(exact_dot(each[t], tails[-1]) if t < times - 1 else each[t])
    tails = tails[::-1]

    for d in range(1, tm):
        @pl.when(mine + d < tm)
        def _(d=d):
            slot = jnp.minimum(mine + d, tm - 1)
            to(product_rows(slot, place), product_rows(slot, place), time_send.at[d],
               time_recv.at[d], tm=slot).wait_recv()
            for e in range(1, team):
                to(product_rows(slot, place), product_rows(slot, place), relay_send.at[d, e],
                   relay_recv.at[d, e], space=base + (place + e) % team).start()
    chains_ref[...] = jnp.concatenate(tails, axis=0)
    for d in range(1, tm):
        @pl.when(mine + d < tm)
        def _(d=d):
            slot = jnp.minimum(mine + d, tm - 1)
            for e in range(1, team):
                origin = (place + team - e) % team
                to(product_rows(slot, origin), product_rows(slot, origin), relay_send.at[d, e],
                   relay_recv.at[d, e], space=base + origin).wait_recv()
            chains_ref[...] = exact_dot(chains_ref[...], products[slot])

    for t in range(times):
        out_ref[t] = chains_ref[t * members:(t + 1) * members].T.astype(out_ref.dtype)

    for copy in sends + shares + partners:
        copy.wait_send()
    for d in range(1, tm):
        @pl.when(mine >= d)
        def _(d=d):
            to(product_rows(mine, place), product_rows(mine, place), time_send.at[d],
               time_recv.at[d], tm=jnp.maximum(mine - d, 0)).wait_send()

        @pl.when(mine + d < tm)
        def _(d=d):
            slot = jnp.minimum(mine + d, tm - 1)
            for e in range(1, team):
                to(product_rows(slot, place), product_rows(slot, place), relay_send.at[d, e],
                   relay_recv.at[d, e], space=base + (place + e) % team).wait_send()


def smooth_kernel(chain_ref, anomalies_ref, out_ref):
    out_ref[0] = jnp.dot(
        chain_ref[0], anomalies_ref[0], preferred_element_type=jnp.float32
    ).astype(out_ref.dtype)


def per_device(space, tm, anomalies, obs_index, obs_weight):
    times, members, cells = anomalies.shape
    obs = obs_index.shape[1]
    whole_vmem = pl.BlockSpec(memory_space=pltpu.VMEM)

    bound = 1.0 + members * obs * space * LARGEST_SCALED**2 / (members - 1)
    steps = math.ceil(math.log(bound / 4.0, 4)) + 3
    rows = times * members // space
    team = space // times
    dma = pltpu.SemaphoreType.DMA
    in_hbm = pl.BlockSpec(memory_space=pltpu.HBM)
    wide = jnp.float32
    square_wide = (members, members)
    chains = pl.pallas_call(
        functools.partial(chain_kernel, space, tm, times, steps),
        in_specs=[in_hbm] * 3,
        out_specs=whole_vmem,
        out_shape=jax.ShapeDtypeStruct((times, members, members), jnp.bfloat16),
        scratch_shapes=[
            pltpu.VMEM(anomalies.shape, anomalies.dtype),
            pltpu.VMEM(obs_index.shape, obs_index.dtype),
            pltpu.VMEM(obs_weight.shape, obs_weight.dtype),
            pltpu.VMEM((times, *square_wide), wide),
            pltpu.VMEM((times - 1, team, rows, members), wide),
            pltpu.VMEM((team, *square_wide), wide),
            pltpu.VMEM(square_wide, wide),
            pltpu.VMEM((times, *square_wide), wide),
            pltpu.VMEM((tm, *square_wide), wide),
            pltpu.VMEM((2 * members, members), wide),
            pltpu.VMEM((times * members, members), wide),
            dma((times,)), dma, dma,
            dma((times, team)), dma((times, team)), dma((team,)), dma((team,)),
            dma((team,)), dma((team,)), dma((times,)), dma((times,)),
            dma((times, team)), dma((times, team)), dma((tm,)), dma((tm,)),
            dma((tm, team)), dma((tm, team)),
        ],
        compiler_params=pltpu.CompilerParams(
            collective_id=0, has_side_effects=True, vmem_limit_bytes=63 * 2**20
        ),
    )(anomalies, obs_index, obs_weight)

    tiles = 2
    tile = pl.BlockSpec((1, members, cells // tiles), lambda t, c: (t, 0, c))
    return pl.pallas_call(
        smooth_kernel,
        grid=(times, tiles),
        in_specs=[pl.BlockSpec((1, members, members), lambda t, c: (t, 0, 0)), tile],
        out_specs=tile,
        out_shape=jax.ShapeDtypeStruct(anomalies.shape, anomalies.dtype),
        compiler_params=pltpu.CompilerParams(vmem_limit_bytes=63 * 2**20),
    )(chains, anomalies)


def solution(mesh):
    return jax.shard_map(
        functools.partial(per_device, mesh.shape["space"], mesh.shape["tm"]),
        mesh=mesh,
        in_specs=(P("tm", None, "space"), P("tm", "space"), P("tm", "space")),
        out_specs=P("tm", None, "space"),
        check_vma=False,
    )
```

```python
import functools
import math

import jax
import jax.numpy as jnp
from jax import lax
from jax.experimental import pallas as pl
from jax.experimental.pallas import tpu as pltpu
from jax.sharding import PartitionSpec as P

MESH = pl.DeviceIdType.MESH
GROUPS = 4
LARGEST_SCALED = 51.0 * 0.12


def split(value):
    high = value.astype(jnp.bfloat16)
    rest = value - high.astype(jnp.float32)
    middle = rest.astype(jnp.bfloat16)
    low = (rest - middle.astype(jnp.float32)).astype(jnp.bfloat16)
    return high, middle, low


def exact_dot(left, right):
    width = right.shape[1]
    left_high, left_middle, left_low = split(left)
    right_high, right_middle, right_low = split(right)
    main_left = jnp.concatenate([left_high, left_middle], axis=1)
    main_row = jnp.concatenate([right_high, right_middle], axis=1)
    main_right = jnp.concatenate([main_row, main_row], axis=0)
    rest_left = jnp.concatenate([left_high, left_low], axis=1)
    rest_right = jnp.concatenate([right_low, right_high], axis=0)
    main = jnp.dot(main_left, main_right, preferred_element_type=jnp.float32)
    rest = jnp.dot(rest_left, rest_right, preferred_element_type=jnp.float32)
    return main[:, :width] + (main[:, width:] + rest)


def gram_of(cells_at, index, weight):
    members, cells = cells_at.shape
    obs = index.shape[1]
    span = cells // GROUPS
    shift = span.bit_length() - 1
    chunk = 256 if obs % 256 == 0 else obs
    low = jnp.bitwise_and(index, span - 1)
    high = lax.shift_right_logical(index, shift)
    stacked = jnp.concatenate(
        [cells_at[:, g * span:(g + 1) * span] for g in range(GROUPS)], axis=0
    )
    cell_ids = lax.broadcasted_iota(jnp.int32, (span, chunk), 0)
    total = jnp.zeros((members, members), jnp.float32)
    for start in range(0, obs, chunk):
        part = slice(start, start + chunk)
        selector = (cell_ids == low[:, part]).astype(jnp.float32).astype(jnp.bfloat16)
        picked = jnp.dot(stacked, selector, preferred_element_type=jnp.float32)
        scaled = jnp.zeros((members, chunk), jnp.float32)
        for g in range(GROUPS):
            group_weight = jnp.where(high[:, part] == g, weight[:, part], 0.0)
            scaled = scaled + picked[g * members:(g + 1) * members] * group_weight
        scaled = scaled.astype(jnp.bfloat16)
        total = total + lax.dot_general(
            scaled, scaled, (((1,), (1,)), ((), ())), preferred_element_type=jnp.float32
        )
    return total


def inverse_of(matrix, identity, steps, both_ref):
    norm = jnp.max(jnp.sum(jnp.abs(matrix), axis=1, keepdims=True), axis=0, keepdims=True)
    least = 1.0 / norm
    size = matrix.shape[0]
    both_ref[:size] = matrix * least
    both_ref[size:] = identity * least

    def step(_, least):
        alpha = 2.0 / (1.0 + least)
        factor = (2.0 * alpha) * identity - (alpha * alpha) * both_ref[:size]
        both_ref[...] = exact_dot(both_ref[...], factor)
        return 4.0 * least / ((1.0 + least) * (1.0 + least))

    lax.fori_loop(0, steps, step, least)
    return both_ref[size:]


def tree(items):
    while len(items) > 1:
        paired = [exact_dot(a, b) for a, b in zip(items[::2], items[1::2])]
        items = paired + items[len(items) - len(items) % 2:]
    return items[0]


def chain_kernel(space, tm, times, steps, anomalies_ref, index_ref, weight_ref, out_ref,
                 cells, index, weight, gram, landed, partner, matrix, weights, products, both_ref, chains_ref,
                 load_sem, index_sem, weight_sem,
                 scatter_send, scatter_recv, partner_send, partner_recv, share_send, share_recv,
                 spread_send, spread_recv, pass_send, pass_recv, time_send, time_recv,
                 relay_send, relay_recv):
    members = matrix.shape[0]
    me = lax.axis_index("space")
    mine = lax.axis_index("tm")
    rows = times * members // space
    team = space // times
    owned = me // team
    place = me % team
    base = owned * team

    def row_slice(number):
        return pl.ds(pl.multiple_of(number * rows, rows), rows)

    def to(source, target, send, recv, **device):
        return pltpu.make_async_remote_copy(
            src_ref=source, dst_ref=target, send_sem=send, recv_sem=recv,
            device_id=device, device_id_type=MESH,
        )

    order = [(owned + 1 + i) % times for i in range(times)]
    index_load = pltpu.make_async_copy(index_ref, index, index_sem)
    weight_load = pltpu.make_async_copy(weight_ref, weight, weight_sem)
    loads = [
        pltpu.make_async_copy(anomalies_ref.at[slot], cells.at[i], load_sem.at[i])
        for i, slot in enumerate(order)
    ]
    index_load.start()
    loads[0].start()
    weight_load.start()
    for load in loads[1:]:
        load.start()

    barrier = pltpu.get_barrier_semaphore()
    for d in range(1, space):
        pl.semaphore_signal(barrier, inc=1, device_id={"space": (me + d) % space}, device_id_type=MESH)
    for d in range(1, tm):
        pl.semaphore_signal(barrier, inc=1, device_id={"tm": (mine + d) % tm}, device_id_type=MESH)
    index_load.wait()
    weight_load.wait()

    sends = []
    for i, slot in enumerate(order):
        loads[i].wait()
        gram[slot] = gram_of(cells.at[i], index[pl.ds(slot, 1), :], weight[pl.ds(slot, 1), :])
        if i == 0:
            pl.semaphore_wait(barrier, space + tm - 2)
        if i < times - 1:
            for e in range(team):
                peer = (place + e) % team
                copy = to(gram.at[slot, row_slice(peer)], landed.at[i, e], scatter_send.at[i, e],
                          scatter_recv.at[i, e], space=slot * team + peer)
                copy.start()
                sends.append(copy)
    partners = []
    for e in range(1, team):
        copy = to(gram.at[owned], partner.at[e], partner_send.at[e], partner_recv.at[e],
                  space=base + (place + e) % team)
        copy.start()
        partners.append(copy)
    for copy in sends:
        copy.wait_recv()
    matrix[row_slice(place), :] = jnp.sum(
        landed[...].reshape((times - 1) * team, rows, members), axis=0
    )
    shares = []
    for e in range(1, team):
        copy = to(matrix.at[row_slice(place)], matrix.at[row_slice(place)], share_send.at[e],
                  share_recv.at[e], space=base + (place + e) % team)
        copy.start()
        shares.append(copy)
    total = gram[owned]
    for copy in partners:
        copy.wait_recv()
    for e in range(1, team):
        total = total + partner[e]
    for e in range(1, team):
        origin = (place + team - e) % team
        to(matrix.at[row_slice(origin)], matrix.at[row_slice(origin)], share_send.at[e],
           share_recv.at[e], space=base + origin).wait_recv()
    total = total + matrix[...]

    identity = (
        lax.broadcasted_iota(jnp.int32, (members, members), 0)
        == lax.broadcasted_iota(jnp.int32, (members, members), 1)
    ).astype(jnp.float32)
    spread = float(members - 1)
    weights[owned] = inverse_of(identity + total / spread, identity, steps, both_ref)

    def own_rows(slot):
        return weights.at[slot, row_slice(place)]

    for d in range(1, times):
        copy = to(own_rows(owned), own_rows(owned), spread_send.at[d], spread_recv.at[d],
                  space=((owned + d) % times) * team + place)
        copy.start()
        sends.append(copy)
    for d in range(1, times):
        slot = (owned + times - d) % times
        to(own_rows(slot), own_rows(slot), spread_send.at[d], spread_recv.at[d],
           space=slot * team + place).wait_recv()
        for e in range(1, team):
            copy = to(own_rows(slot), own_rows(slot), pass_send.at[d, e], pass_recv.at[d, e],
                      space=base + (place + e) % team)
            copy.start()
            sends.append(copy)
    for d in range(1, times):
        slot = (owned + times - d) % times
        for e in range(1, team):
            origin = (place + team - e) % team
            there = weights.at[slot, row_slice(origin)]
            to(there, there, pass_send.at[d, e], pass_recv.at[d, e], space=base + origin).wait_recv()

    each = [weights[t] for t in range(times)]
    products[mine] = tree(each)

    def product_rows(slot, number):
        return products.at[slot, row_slice(number)]

    for d in range(1, tm):
        @pl.when(mine >= d)
        def _(d=d):
            to(product_rows(mine, place), product_rows(mine, place), time_send.at[d],
               time_recv.at[d], tm=jnp.maximum(mine - d, 0)).start()

    tails = [identity]
    for t in range(times - 1, 0, -1):
        tails.append(exact_dot(each[t], tails[-1]) if t < times - 1 else each[t])
    tails = tails[::-1]

    for d in range(1, tm):
        @pl.when(mine + d < tm)
        def _(d=d):
            slot = jnp.minimum(mine + d, tm - 1)
            to(product_rows(slot, place), product_rows(slot, place), time_send.at[d],
               time_recv.at[d], tm=slot).wait_recv()
            for e in range(1, team):
                to(product_rows(slot, place), product_rows(slot, place), relay_send.at[d, e],
                   relay_recv.at[d, e], space=base + (place + e) % team).start()
    chains_ref[...] = jnp.concatenate(tails, axis=0)
    for d in range(1, tm):
        @pl.when(mine + d < tm)
        def _(d=d):
            slot = jnp.minimum(mine + d, tm - 1)
            for e in range(1, team):
                origin = (place + team - e) % team
                to(product_rows(slot, origin), product_rows(slot, origin), relay_send.at[d, e],
                   relay_recv.at[d, e], space=base + origin).wait_recv()
            chains_ref[...] = exact_dot(chains_ref[...], products[slot])

    for t in range(times):
        out_ref[t] = chains_ref[t * members:(t + 1) * members].T.astype(out_ref.dtype)

    for copy in sends + shares + partners:
        copy.wait_send()
    for d in range(1, tm):
        @pl.when(mine >= d)
        def _(d=d):
            to(product_rows(mine, place), product_rows(mine, place), time_send.at[d],
               time_recv.at[d], tm=jnp.maximum(mine - d, 0)).wait_send()

        @pl.when(mine + d < tm)
        def _(d=d):
            slot = jnp.minimum(mine + d, tm - 1)
            for e in range(1, team):
                to(product_rows(slot, place), product_rows(slot, place), relay_send.at[d, e],
                   relay_recv.at[d, e], space=base + (place + e) % team).wait_send()


def smooth_kernel(chain_ref, anomalies_ref, out_ref, done, done_sem):
    times, members, cells = anomalies_ref.shape
    parts = done_sem.shape[1]
    width = cells // parts
    copies = []
    for t in range(times):
        for c in range(parts):
            part = slice(c * width, (c + 1) * width)
            done[t, :, part] = jnp.dot(
                chain_ref[t], anomalies_ref[t, :, part], preferred_element_type=jnp.float32
            ).astype(done.dtype)
            copy = pltpu.make_async_copy(
                done.at[t, :, part], out_ref.at[t, :, part], done_sem.at[t, c]
            )
            copy.start()
            copies.append(copy)
    for copy in copies:
        copy.wait()


def per_device(space, tm, anomalies, obs_index, obs_weight):
    times, members, cells = anomalies.shape
    obs = obs_index.shape[1]
    whole_vmem = pl.BlockSpec(memory_space=pltpu.VMEM)

    bound = 1.0 + members * obs * space * LARGEST_SCALED**2 / (members - 1)
    steps = math.ceil(math.log(bound / 4.0, 4)) + 3
    rows = times * members // space
    team = space // times
    dma = pltpu.SemaphoreType.DMA
    in_hbm = pl.BlockSpec(memory_space=pltpu.HBM)
    wide = jnp.float32
    square_wide = (members, members)
    chains = pl.pallas_call(
        functools.partial(chain_kernel, space, tm, times, steps),
        in_specs=[in_hbm] * 3,
        out_specs=whole_vmem,
        out_shape=jax.ShapeDtypeStruct((times, members, members), jnp.bfloat16),
        scratch_shapes=[
            pltpu.VMEM(anomalies.shape, anomalies.dtype),
            pltpu.VMEM(obs_index.shape, obs_index.dtype),
            pltpu.VMEM(obs_weight.shape, obs_weight.dtype),
            pltpu.VMEM((times, *square_wide), wide),
            pltpu.VMEM((times - 1, team, rows, members), wide),
            pltpu.VMEM((team, *square_wide), wide),
            pltpu.VMEM(square_wide, wide),
            pltpu.VMEM((times, *square_wide), wide),
            pltpu.VMEM((tm, *square_wide), wide),
            pltpu.VMEM((2 * members, members), wide),
            pltpu.VMEM((times * members, members), wide),
            dma((times,)), dma, dma,
            dma((times, team)), dma((times, team)), dma((team,)), dma((team,)),
            dma((team,)), dma((team,)), dma((times,)), dma((times,)),
            dma((times, team)), dma((times, team)), dma((tm,)), dma((tm,)),
            dma((tm, team)), dma((tm, team)),
        ],
        compiler_params=pltpu.CompilerParams(
            collective_id=0, has_side_effects=True, vmem_limit_bytes=40 * 2**20
        ),
    )(*(pltpu.with_memory_space_constraint(x, pltpu.HBM) for x in (anomalies, obs_index, obs_weight)))

    return pl.pallas_call(
        smooth_kernel,
        in_specs=[whole_vmem, whole_vmem],
        out_specs=in_hbm,
        out_shape=jax.ShapeDtypeStruct(anomalies.shape, anomalies.dtype),
        scratch_shapes=[pltpu.VMEM(anomalies.shape, anomalies.dtype), dma((times, 2))],
        compiler_params=pltpu.CompilerParams(vmem_limit_bytes=40 * 2**20),
    )(chains, anomalies)


def solution(mesh):
    return jax.shard_map(
        functools.partial(per_device, mesh.shape["space"], mesh.shape["tm"]),
        mesh=mesh,
        in_specs=(P("tm", None, "space"), P("tm", "space"), P("tm", "space")),
        out_specs=P("tm", None, "space"),
        check_vma=False,
    )
```

```python
import functools
import math

import jax
import jax.numpy as jnp
from jax import lax
from jax.experimental import pallas as pl
from jax.experimental.pallas import tpu as pltpu
from jax.sharding import PartitionSpec as P

MESH = pl.DeviceIdType.MESH
LANES = 128
LARGEST_SCALED = 51.0 * 0.12


def split(value):
    high = value.astype(jnp.bfloat16)
    rest = value - high.astype(jnp.float32)
    middle = rest.astype(jnp.bfloat16)
    low = (rest - middle.astype(jnp.float32)).astype(jnp.bfloat16)
    return high, middle, low


def exact_dot(left, right):
    width = right.shape[1]
    left_high, left_middle, left_low = split(left)
    right_high, right_middle, right_low = split(right)
    main_left = jnp.concatenate([left_high, left_middle], axis=1)
    main_row = jnp.concatenate([right_high, right_middle], axis=1)
    main_right = jnp.concatenate([main_row, main_row], axis=0)
    rest_left = jnp.concatenate([left_high, left_low], axis=1)
    rest_right = jnp.concatenate([right_low, right_high], axis=0)
    main = jnp.dot(main_left, main_right, preferred_element_type=jnp.float32)
    rest = jnp.dot(rest_left, rest_right, preferred_element_type=jnp.float32)
    return main[:, :width] + (main[:, width:] + rest)


def cell_roots(index, weight, cells):
    low = jnp.bitwise_and(index, LANES - 1)
    high = lax.shift_right_logical(index, LANES.bit_length() - 1)
    groups = cells // LANES
    obs = index.shape[1]
    square = weight * weight
    coarse = square.astype(jnp.bfloat16).astype(jnp.float32)
    in_group = lax.broadcasted_iota(jnp.int32, (groups, obs), 0) == high
    left = jnp.concatenate(
        [jnp.where(in_group, coarse, 0.0), jnp.where(in_group, square - coarse, 0.0)], axis=0
    ).astype(jnp.bfloat16)
    right = (lax.broadcasted_iota(jnp.int32, (LANES, obs), 0) == low)
    right = right.astype(jnp.float32).astype(jnp.bfloat16)
    both = lax.dot_general(
        left, right, (((1,), (1,)), ((), ())), preferred_element_type=jnp.float32
    )
    return jnp.sqrt(both[:groups] + both[groups:])


def gram_of(cells_at, roots):
    groups = roots.shape[0]
    scaled = jnp.concatenate(
        [
            (cells_at[:, g * LANES:(g + 1) * LANES].astype(jnp.float32) * roots[g:g + 1])
            .astype(jnp.bfloat16)
            for g in range(groups)
        ],
        axis=1,
    )
    return lax.dot_general(
        scaled, scaled, (((1,), (1,)), ((), ())), preferred_element_type=jnp.float32
    )


def inverse_of(matrix, identity, steps, both_ref):
    norm = jnp.max(jnp.sum(jnp.abs(matrix), axis=1, keepdims=True), axis=0, keepdims=True)
    least = 1.0 / norm
    size = matrix.shape[0]
    both_ref[:size] = matrix * least
    both_ref[size:] = identity * least

    def step(_, least):
        alpha = 2.0 / (1.0 + least)
        factor = (2.0 * alpha) * identity - (alpha * alpha) * both_ref[:size]
        both_ref[...] = exact_dot(both_ref[...], factor)
        return 4.0 * least / ((1.0 + least) * (1.0 + least))

    lax.fori_loop(0, steps, step, least)
    return both_ref[size:]


def tree(items):
    while len(items) > 1:
        paired = [exact_dot(a, b) for a, b in zip(items[::2], items[1::2])]
        items = paired + items[len(items) - len(items) % 2:]
    return items[0]


def chain_kernel(space, tm, times, steps, anomalies_ref, index_ref, weight_ref, out_ref,
                 cells, index, weight, gram, landed, partner, matrix, weights, products, both_ref, chains_ref,
                 load_sem, index_sem, weight_sem,
                 scatter_send, scatter_recv, partner_send, partner_recv, share_send, share_recv,
                 spread_send, spread_recv, pass_send, pass_recv, time_send, time_recv,
                 relay_send, relay_recv):
    members = matrix.shape[0]
    me = lax.axis_index("space")
    mine = lax.axis_index("tm")
    rows = times * members // space
    team = space // times
    owned = me // team
    place = me % team
    base = owned * team

    def row_slice(number):
        return pl.ds(pl.multiple_of(number * rows, rows), rows)

    def to(source, target, send, recv, **device):
        return pltpu.make_async_remote_copy(
            src_ref=source, dst_ref=target, send_sem=send, recv_sem=recv,
            device_id=device, device_id_type=MESH,
        )

    order = [(owned + 1 + i) % times for i in range(times)]
    index_load = pltpu.make_async_copy(index_ref, index, index_sem)
    weight_load = pltpu.make_async_copy(weight_ref, weight, weight_sem)
    loads = [
        pltpu.make_async_copy(anomalies_ref.at[slot], cells.at[i], load_sem.at[i])
        for i, slot in enumerate(order)
    ]
    index_load.start()
    loads[0].start()
    weight_load.start()
    for load in loads[1:]:
        load.start()

    barrier = pltpu.get_barrier_semaphore()
    for d in range(1, space):
        pl.semaphore_signal(barrier, inc=1, device_id={"space": (me + d) % space}, device_id_type=MESH)
    for d in range(1, tm):
        pl.semaphore_signal(barrier, inc=1, device_id={"tm": (mine + d) % tm}, device_id_type=MESH)
    index_load.wait()
    weight_load.wait()

    sends = []
    roots = [
        cell_roots(index[pl.ds(slot, 1), :], weight[pl.ds(slot, 1), :], cells.shape[2])
        for slot in order
    ]
    for i, slot in enumerate(order):
        loads[i].wait()
        gram[slot] = gram_of(cells.at[i], roots[i])
        if i == 0:
            pl.semaphore_wait(barrier, space + tm - 2)
        if i < times - 1:
            for e in range(team):
                peer = (place + e) % team
                copy = to(gram.at[slot, row_slice(peer)], landed.at[i, e], scatter_send.at[i, e],
                          scatter_recv.at[i, e], space=slot * team + peer)
                copy.start()
                sends.append(copy)
    partners = []
    for e in range(1, team):
        copy = to(gram.at[owned], partner.at[e], partner_send.at[e], partner_recv.at[e],
                  space=base + (place + e) % team)
        copy.start()
        partners.append(copy)
    for copy in sends:
        copy.wait_recv()
    matrix[row_slice(place), :] = jnp.sum(
        landed[...].reshape((times - 1) * team, rows, members), axis=0
    )
    shares = []
    for e in range(1, team):
        copy = to(matrix.at[row_slice(place)], matrix.at[row_slice(place)], share_send.at[e],
                  share_recv.at[e], space=base + (place + e) % team)
        copy.start()
        shares.append(copy)
    total = gram[owned]
    for copy in partners:
        copy.wait_recv()
    for e in range(1, team):
        total = total + partner[e]
    for e in range(1, team):
        origin = (place + team - e) % team
        to(matrix.at[row_slice(origin)], matrix.at[row_slice(origin)], share_send.at[e],
           share_recv.at[e], space=base + origin).wait_recv()
    total = total + matrix[...]

    identity = (
        lax.broadcasted_iota(jnp.int32, (members, members), 0)
        == lax.broadcasted_iota(jnp.int32, (members, members), 1)
    ).astype(jnp.float32)
    spread = float(members - 1)
    weights[owned] = inverse_of(identity + total / spread, identity, steps, both_ref)

    def own_rows(slot):
        return weights.at[slot, row_slice(place)]

    for d in range(1, times):
        copy = to(own_rows(owned), own_rows(owned), spread_send.at[d], spread_recv.at[d],
                  space=((owned + d) % times) * team + place)
        copy.start()
        sends.append(copy)
    for d in range(1, times):
        slot = (owned + times - d) % times
        to(own_rows(slot), own_rows(slot), spread_send.at[d], spread_recv.at[d],
           space=slot * team + place).wait_recv()
        for e in range(1, team):
            copy = to(own_rows(slot), own_rows(slot), pass_send.at[d, e], pass_recv.at[d, e],
                      space=base + (place + e) % team)
            copy.start()
            sends.append(copy)
    for d in range(1, times):
        slot = (owned + times - d) % times
        for e in range(1, team):
            origin = (place + team - e) % team
            there = weights.at[slot, row_slice(origin)]
            to(there, there, pass_send.at[d, e], pass_recv.at[d, e], space=base + origin).wait_recv()

    each = [weights[t] for t in range(times)]
    products[mine] = tree(each)

    def product_rows(slot, number):
        return products.at[slot, row_slice(number)]

    for d in range(1, tm):
        @pl.when(mine >= d)
        def _(d=d):
            to(product_rows(mine, place), product_rows(mine, place), time_send.at[d],
               time_recv.at[d], tm=jnp.maximum(mine - d, 0)).start()

    tails = [identity]
    for t in range(times - 1, 0, -1):
        tails.append(exact_dot(each[t], tails[-1]) if t < times - 1 else each[t])
    tails = tails[::-1]

    for d in range(1, tm):
        @pl.when(mine + d < tm)
        def _(d=d):
            slot = jnp.minimum(mine + d, tm - 1)
            to(product_rows(slot, place), product_rows(slot, place), time_send.at[d],
               time_recv.at[d], tm=slot).wait_recv()
            for e in range(1, team):
                to(product_rows(slot, place), product_rows(slot, place), relay_send.at[d, e],
                   relay_recv.at[d, e], space=base + (place + e) % team).start()
    chains_ref[...] = jnp.concatenate(tails, axis=0)
    for d in range(1, tm):
        @pl.when(mine + d < tm)
        def _(d=d):
            slot = jnp.minimum(mine + d, tm - 1)
            for e in range(1, team):
                origin = (place + team - e) % team
                to(product_rows(slot, origin), product_rows(slot, origin), relay_send.at[d, e],
                   relay_recv.at[d, e], space=base + origin).wait_recv()
            chains_ref[...] = exact_dot(chains_ref[...], products[slot])

    for t in range(times):
        out_ref[t] = chains_ref[t * members:(t + 1) * members].T.astype(out_ref.dtype)

    for copy in sends + shares + partners:
        copy.wait_send()
    for d in range(1, tm):
        @pl.when(mine >= d)
        def _(d=d):
            to(product_rows(mine, place), product_rows(mine, place), time_send.at[d],
               time_recv.at[d], tm=jnp.maximum(mine - d, 0)).wait_send()

        @pl.when(mine + d < tm)
        def _(d=d):
            slot = jnp.minimum(mine + d, tm - 1)
            for e in range(1, team):
                to(product_rows(slot, place), product_rows(slot, place), relay_send.at[d, e],
                   relay_recv.at[d, e], space=base + (place + e) % team).wait_send()


def smooth_kernel(chain_ref, anomalies_ref, out_ref, done, done_sem):
    times, members, cells = anomalies_ref.shape
    parts = done_sem.shape[1]
    width = cells // parts
    copies = []
    for t in range(times):
        for c in range(parts):
            part = slice(c * width, (c + 1) * width)
            done[t, :, part] = jnp.dot(
                chain_ref[t], anomalies_ref[t, :, part], preferred_element_type=jnp.float32
            ).astype(done.dtype)
            copy = pltpu.make_async_copy(
                done.at[t, :, part], out_ref.at[t, :, part], done_sem.at[t, c]
            )
            copy.start()
            copies.append(copy)
    for copy in copies:
        copy.wait()


def per_device(space, tm, anomalies, obs_index, obs_weight):
    times, members, cells = anomalies.shape
    obs = obs_index.shape[1]
    whole_vmem = pl.BlockSpec(memory_space=pltpu.VMEM)

    bound = 1.0 + members * obs * space * LARGEST_SCALED**2 / (members - 1)
    steps = math.ceil(math.log(bound / 4.0, 4)) + 3
    rows = times * members // space
    team = space // times
    dma = pltpu.SemaphoreType.DMA
    in_hbm = pl.BlockSpec(memory_space=pltpu.HBM)
    wide = jnp.float32
    square_wide = (members, members)
    chains = pl.pallas_call(
        functools.partial(chain_kernel, space, tm, times, steps),
        in_specs=[in_hbm] * 3,
        out_specs=whole_vmem,
        out_shape=jax.ShapeDtypeStruct((times, members, members), jnp.bfloat16),
        scratch_shapes=[
            pltpu.VMEM(anomalies.shape, anomalies.dtype),
            pltpu.VMEM(obs_index.shape, obs_index.dtype),
            pltpu.VMEM(obs_weight.shape, obs_weight.dtype),
            pltpu.VMEM((times, *square_wide), wide),
            pltpu.VMEM((times - 1, team, rows, members), wide),
            pltpu.VMEM((team, *square_wide), wide),
            pltpu.VMEM(square_wide, wide),
            pltpu.VMEM((times, *square_wide), wide),
            pltpu.VMEM((tm, *square_wide), wide),
            pltpu.VMEM((2 * members, members), wide),
            pltpu.VMEM((times * members, members), wide),
            dma((times,)), dma, dma,
            dma((times, team)), dma((times, team)), dma((team,)), dma((team,)),
            dma((team,)), dma((team,)), dma((times,)), dma((times,)),
            dma((times, team)), dma((times, team)), dma((tm,)), dma((tm,)),
            dma((tm, team)), dma((tm, team)),
        ],
        compiler_params=pltpu.CompilerParams(
            collective_id=0, has_side_effects=True, vmem_limit_bytes=40 * 2**20
        ),
    )(*(pltpu.with_memory_space_constraint(x, pltpu.HBM) for x in (anomalies, obs_index, obs_weight)))

    return pl.pallas_call(
        smooth_kernel,
        in_specs=[whole_vmem, whole_vmem],
        out_specs=in_hbm,
        out_shape=jax.ShapeDtypeStruct(anomalies.shape, anomalies.dtype),
        scratch_shapes=[pltpu.VMEM(anomalies.shape, anomalies.dtype), dma((times, 2))],
        compiler_params=pltpu.CompilerParams(vmem_limit_bytes=40 * 2**20),
    )(chains, anomalies)


def solution(mesh):
    return jax.shard_map(
        functools.partial(per_device, mesh.shape["space"], mesh.shape["tm"]),
        mesh=mesh,
        in_specs=(P("tm", None, "space"), P("tm", "space"), P("tm", "space")),
        out_specs=P("tm", None, "space"),
        check_vma=False,
    )
```

```python
import functools
import math

import jax
import jax.numpy as jnp
from jax import lax
from jax.experimental import pallas as pl
from jax.experimental.pallas import tpu as pltpu
from jax.sharding import PartitionSpec as P

MESH = pl.DeviceIdType.MESH
LANES = 128
LARGEST_SCALED = 51.0 * 0.12


def split(value):
    high = value.astype(jnp.bfloat16)
    rest = value - high.astype(jnp.float32)
    middle = rest.astype(jnp.bfloat16)
    low = (rest - middle.astype(jnp.float32)).astype(jnp.bfloat16)
    return high, middle, low


def exact_dot(left, right):
    width = right.shape[1]
    left_high, left_middle, left_low = split(left)
    right_high, right_middle, right_low = split(right)
    main_left = jnp.concatenate([left_high, left_middle], axis=1)
    main_row = jnp.concatenate([right_high, right_middle], axis=1)
    main_right = jnp.concatenate([main_row, main_row], axis=0)
    rest_left = jnp.concatenate([left_high, left_low], axis=1)
    rest_right = jnp.concatenate([right_low, right_high], axis=0)
    main = jnp.dot(main_left, main_right, preferred_element_type=jnp.float32)
    rest = jnp.dot(rest_left, rest_right, preferred_element_type=jnp.float32)
    return main[:, :width] + (main[:, width:] + rest)


def cell_roots(index, weight, cells):
    low = jnp.bitwise_and(index, LANES - 1)
    high = lax.shift_right_logical(index, LANES.bit_length() - 1)
    groups = cells // LANES
    obs = index.shape[1]
    square = weight * weight
    coarse = square.astype(jnp.bfloat16).astype(jnp.float32)
    in_group = lax.broadcasted_iota(jnp.int32, (groups, obs), 0) == high
    left = jnp.concatenate(
        [jnp.where(in_group, coarse, 0.0), jnp.where(in_group, square - coarse, 0.0)], axis=0
    ).astype(jnp.bfloat16)
    right = (lax.broadcasted_iota(jnp.int32, (LANES, obs), 0) == low)
    right = right.astype(jnp.float32).astype(jnp.bfloat16)
    both = lax.dot_general(
        left, right, (((1,), (1,)), ((), ())), preferred_element_type=jnp.float32
    )
    return jnp.sqrt(both[:groups] + both[groups:])


def gram_of(cells_at, roots):
    groups = roots.shape[0]
    scaled = jnp.concatenate(
        [
            (cells_at[:, g * LANES:(g + 1) * LANES].astype(jnp.float32) * roots[g:g + 1])
            .astype(jnp.bfloat16)
            for g in range(groups)
        ],
        axis=1,
    )
    return lax.dot_general(
        scaled, scaled, (((1,), (1,)), ((), ())), preferred_element_type=jnp.float32
    )


def inverse_of(matrix, identity, steps, both_ref):
    norm = jnp.max(jnp.sum(jnp.abs(matrix), axis=1, keepdims=True), axis=0, keepdims=True)
    least = 1.0 / norm
    size = matrix.shape[0]
    both_ref[:size] = matrix * least
    both_ref[size:] = identity * least

    def step(_, least):
        alpha = 2.0 / (1.0 + least)
        factor = (2.0 * alpha) * identity - (alpha * alpha) * both_ref[:size]
        both_ref[...] = exact_dot(both_ref[...], factor)
        return 4.0 * least / ((1.0 + least) * (1.0 + least))

    lax.fori_loop(0, steps, step, least)
    return both_ref[size:]


def tree(items):
    while len(items) > 1:
        paired = [exact_dot(a, b) for a, b in zip(items[::2], items[1::2])]
        items = paired + items[len(items) - len(items) % 2:]
    return items[0]


def chain_kernel(space, tm, times, steps, anomalies_ref, index_ref, weight_ref, out_ref,
                 cells, index, weight, gram, near, joint, far, partner, matrix, weights, products, both_ref, chains_ref,
                 load_sem, index_sem, weight_sem,
                 near_send, near_recv, far_send, far_recv, partner_send, partner_recv, share_send, share_recv,
                 spread_send, spread_recv, pass_send, pass_recv, time_send, time_recv,
                 relay_send, relay_recv):
    members = matrix.shape[0]
    me = lax.axis_index("space")
    mine = lax.axis_index("tm")
    rows = times * members // space
    team = space // times
    owned = me // team
    place = me % team
    base = owned * team

    def row_slice(number):
        return pl.ds(pl.multiple_of(number * rows, rows), rows)

    def to(source, target, send, recv, **device):
        return pltpu.make_async_remote_copy(
            src_ref=source, dst_ref=target, send_sem=send, recv_sem=recv,
            device_id=device, device_id_type=MESH,
        )

    order = [(owned + 1 + i) % times for i in range(times)]
    index_load = pltpu.make_async_copy(index_ref, index, index_sem)
    weight_load = pltpu.make_async_copy(weight_ref, weight, weight_sem)
    loads = [
        pltpu.make_async_copy(anomalies_ref.at[slot], cells.at[i], load_sem.at[i])
        for i, slot in enumerate(order)
    ]
    index_load.start()
    loads[0].start()
    weight_load.start()
    for load in loads[1:]:
        load.start()

    barrier = pltpu.get_barrier_semaphore()
    for d in range(1, space):
        pl.semaphore_signal(barrier, inc=1, device_id={"space": (me + d) % space}, device_id_type=MESH)
    for d in range(1, tm):
        pl.semaphore_signal(barrier, inc=1, device_id={"tm": (mine + d) % tm}, device_id_type=MESH)
    index_load.wait()
    weight_load.wait()

    sends = []
    near_copies = []
    far_copies = []

    def pass_on(i):
        piece = gram[order[i], row_slice(place), :]
        for copy in near_copies[i]:
            copy.wait_recv()
        for e in range(1, team):
            piece = piece + near[i, e]
        joint[i] = piece
        copy = to(joint.at[i], far.at[i], far_send.at[i], far_recv.at[i],
                  space=order[i] * team + place)
        copy.start()
        far_copies.append(copy)

    roots = [
        cell_roots(index[pl.ds(slot, 1), :], weight[pl.ds(slot, 1), :], cells.shape[2])
        for slot in order
    ]
    for i, slot in enumerate(order):
        loads[i].wait()
        gram[slot] = gram_of(cells.at[i], roots[i])
        if i == 0:
            pl.semaphore_wait(barrier, space + tm - 2)
        if i < times - 1:
            near_copies.append([])
            for e in range(1, team):
                peer = (place + e) % team
                copy = to(gram.at[slot, row_slice(peer)], near.at[i, e], near_send.at[i, e],
                          near_recv.at[i, e], space=base + peer)
                copy.start()
                near_copies[i].append(copy)
        if 2 <= i < times - 1:
            pass_on(i - 2)
    partners = []
    for e in range(1, team):
        copy = to(gram.at[owned], partner.at[e], partner_send.at[e], partner_recv.at[e],
                  space=base + (place + e) % team)
        copy.start()
        partners.append(copy)
    for i in range(max(times - 3, 0), times - 1):
        pass_on(i)
    for copy in far_copies:
        copy.wait_recv()
    matrix[row_slice(place), :] = jnp.sum(far[...], axis=0)
    shares = []
    for e in range(1, team):
        copy = to(matrix.at[row_slice(place)], matrix.at[row_slice(place)], share_send.at[e],
                  share_recv.at[e], space=base + (place + e) % team)
        copy.start()
        shares.append(copy)
    total = gram[owned]
    for copy in partners:
        copy.wait_recv()
    for e in range(1, team):
        total = total + partner[e]
    for e in range(1, team):
        origin = (place + team - e) % team
        to(matrix.at[row_slice(origin)], matrix.at[row_slice(origin)], share_send.at[e],
           share_recv.at[e], space=base + origin).wait_recv()
    total = total + matrix[...]

    identity = (
        lax.broadcasted_iota(jnp.int32, (members, members), 0)
        == lax.broadcasted_iota(jnp.int32, (members, members), 1)
    ).astype(jnp.float32)
    spread = float(members - 1)
    weights[owned] = inverse_of(identity + total / spread, identity, steps, both_ref)

    def own_rows(slot):
        return weights.at[slot, row_slice(place)]

    for d in range(1, times):
        copy = to(own_rows(owned), own_rows(owned), spread_send.at[d], spread_recv.at[d],
                  space=((owned + d) % times) * team + place)
        copy.start()
        sends.append(copy)
    for d in range(1, times):
        slot = (owned + times - d) % times
        to(own_rows(slot), own_rows(slot), spread_send.at[d], spread_recv.at[d],
           space=slot * team + place).wait_recv()
        for e in range(1, team):
            copy = to(own_rows(slot), own_rows(slot), pass_send.at[d, e], pass_recv.at[d, e],
                      space=base + (place + e) % team)
            copy.start()
            sends.append(copy)
    for d in range(1, times):
        slot = (owned + times - d) % times
        for e in range(1, team):
            origin = (place + team - e) % team
            there = weights.at[slot, row_slice(origin)]
            to(there, there, pass_send.at[d, e], pass_recv.at[d, e], space=base + origin).wait_recv()

    each = [weights[t] for t in range(times)]
    products[mine] = tree(each)

    def product_rows(slot, number):
        return products.at[slot, row_slice(number)]

    for d in range(1, tm):
        @pl.when(mine >= d)
        def _(d=d):
            to(product_rows(mine, place), product_rows(mine, place), time_send.at[d],
               time_recv.at[d], tm=jnp.maximum(mine - d, 0)).start()

    tails = [identity]
    for t in range(times - 1, 0, -1):
        tails.append(exact_dot(each[t], tails[-1]) if t < times - 1 else each[t])
    tails = tails[::-1]

    for d in range(1, tm):
        @pl.when(mine + d < tm)
        def _(d=d):
            slot = jnp.minimum(mine + d, tm - 1)
            to(product_rows(slot, place), product_rows(slot, place), time_send.at[d],
               time_recv.at[d], tm=slot).wait_recv()
            for e in range(1, team):
                to(product_rows(slot, place), product_rows(slot, place), relay_send.at[d, e],
                   relay_recv.at[d, e], space=base + (place + e) % team).start()
    chains_ref[...] = jnp.concatenate(tails, axis=0)
    for d in range(1, tm):
        @pl.when(mine + d < tm)
        def _(d=d):
            slot = jnp.minimum(mine + d, tm - 1)
            for e in range(1, team):
                origin = (place + team - e) % team
                to(product_rows(slot, origin), product_rows(slot, origin), relay_send.at[d, e],
                   relay_recv.at[d, e], space=base + origin).wait_recv()
            chains_ref[...] = exact_dot(chains_ref[...], products[slot])

    for t in range(times):
        out_ref[t] = chains_ref[t * members:(t + 1) * members].T.astype(out_ref.dtype)

    for copy in sum(near_copies, sends + shares + partners + far_copies):
        copy.wait_send()
    for d in range(1, tm):
        @pl.when(mine >= d)
        def _(d=d):
            to(product_rows(mine, place), product_rows(mine, place), time_send.at[d],
               time_recv.at[d], tm=jnp.maximum(mine - d, 0)).wait_send()

        @pl.when(mine + d < tm)
        def _(d=d):
            slot = jnp.minimum(mine + d, tm - 1)
            for e in range(1, team):
                to(product_rows(slot, place), product_rows(slot, place), relay_send.at[d, e],
                   relay_recv.at[d, e], space=base + (place + e) % team).wait_send()


def smooth_kernel(chain_ref, anomalies_ref, out_ref, done, done_sem):
    times, members, cells = anomalies_ref.shape
    parts = done_sem.shape[1]
    width = cells // parts
    copies = []
    for t in range(times):
        for c in range(parts):
            part = slice(c * width, (c + 1) * width)
            done[t, :, part] = jnp.dot(
                chain_ref[t], anomalies_ref[t, :, part], preferred_element_type=jnp.float32
            ).astype(done.dtype)
            copy = pltpu.make_async_copy(
                done.at[t, :, part], out_ref.at[t, :, part], done_sem.at[t, c]
            )
            copy.start()
            copies.append(copy)
    for copy in copies:
        copy.wait()


def per_device(space, tm, anomalies, obs_index, obs_weight):
    times, members, cells = anomalies.shape
    obs = obs_index.shape[1]
    whole_vmem = pl.BlockSpec(memory_space=pltpu.VMEM)

    bound = 1.0 + members * obs * space * LARGEST_SCALED**2 / (members - 1)
    steps = math.ceil(math.log(bound / 4.0, 4)) + 3
    rows = times * members // space
    team = space // times
    dma = pltpu.SemaphoreType.DMA
    in_hbm = pl.BlockSpec(memory_space=pltpu.HBM)
    wide = jnp.float32
    square_wide = (members, members)
    chains = pl.pallas_call(
        functools.partial(chain_kernel, space, tm, times, steps),
        in_specs=[in_hbm] * 3,
        out_specs=whole_vmem,
        out_shape=jax.ShapeDtypeStruct((times, members, members), jnp.bfloat16),
        scratch_shapes=[
            pltpu.VMEM(anomalies.shape, anomalies.dtype),
            pltpu.VMEM(obs_index.shape, obs_index.dtype),
            pltpu.VMEM(obs_weight.shape, obs_weight.dtype),
            pltpu.VMEM((times, *square_wide), wide),
            pltpu.VMEM((times - 1, team, rows, members), wide),
            pltpu.VMEM((times - 1, rows, members), wide),
            pltpu.VMEM((times - 1, rows, members), wide),
            pltpu.VMEM((team, *square_wide), wide),
            pltpu.VMEM(square_wide, wide),
            pltpu.VMEM((times, *square_wide), wide),
            pltpu.VMEM((tm, *square_wide), wide),
            pltpu.VMEM((2 * members, members), wide),
            pltpu.VMEM((times * members, members), wide),
            dma((times,)), dma, dma,
            dma((times, team)), dma((times, team)), dma((times,)), dma((times,)), dma((team,)), dma((team,)),
            dma((team,)), dma((team,)), dma((times,)), dma((times,)),
            dma((times, team)), dma((times, team)), dma((tm,)), dma((tm,)),
            dma((tm, team)), dma((tm, team)),
        ],
        compiler_params=pltpu.CompilerParams(
            collective_id=0, has_side_effects=True, vmem_limit_bytes=40 * 2**20
        ),
    )(*(pltpu.with_memory_space_constraint(x, pltpu.HBM) for x in (anomalies, obs_index, obs_weight)))

    return pl.pallas_call(
        smooth_kernel,
        in_specs=[whole_vmem, whole_vmem],
        out_specs=in_hbm,
        out_shape=jax.ShapeDtypeStruct(anomalies.shape, anomalies.dtype),
        scratch_shapes=[pltpu.VMEM(anomalies.shape, anomalies.dtype), dma((times, 2))],
        compiler_params=pltpu.CompilerParams(vmem_limit_bytes=40 * 2**20),
    )(chains, anomalies)


def solution(mesh):
    return jax.shard_map(
        functools.partial(per_device, mesh.shape["space"], mesh.shape["tm"]),
        mesh=mesh,
        in_specs=(P("tm", None, "space"), P("tm", "space"), P("tm", "space")),
        out_specs=P("tm", None, "space"),
        check_vma=False,
    )
```

```python
import functools
import math

import jax
import jax.numpy as jnp
from jax import lax
from jax.experimental import pallas as pl
from jax.experimental.pallas import tpu as pltpu
from jax.sharding import PartitionSpec as P

MESH = pl.DeviceIdType.MESH
LANES = 128
LARGEST_SCALED = 51.0 * 0.12


def split(value):
    high = value.astype(jnp.bfloat16)
    rest = value - high.astype(jnp.float32)
    return high, rest.astype(jnp.bfloat16), rest


def near_dot(left, right):
    width = right.shape[1]
    left_high, left_middle, _ = split(left)
    right_high, right_middle, _ = split(right)
    main_left = jnp.concatenate([left_high, left_middle], axis=1)
    main_row = jnp.concatenate([right_high, right_middle], axis=1)
    main_right = jnp.concatenate([main_row, main_row], axis=0)
    main = jnp.dot(main_left, main_right, preferred_element_type=jnp.float32)
    return main[:, :width] + main[:, width:]


def exact_dot(left, right):
    width = right.shape[1]
    left_high, left_middle, left_rest = split(left)
    right_high, right_middle, right_rest = split(right)
    left_low = (left_rest - left_middle.astype(jnp.float32)).astype(jnp.bfloat16)
    right_low = (right_rest - right_middle.astype(jnp.float32)).astype(jnp.bfloat16)
    main_left = jnp.concatenate([left_high, left_middle], axis=1)
    main_row = jnp.concatenate([right_high, right_middle], axis=1)
    main_right = jnp.concatenate([main_row, main_row], axis=0)
    rest_left = jnp.concatenate([left_high, left_low], axis=1)
    rest_right = jnp.concatenate([right_low, right_high], axis=0)
    main = jnp.dot(main_left, main_right, preferred_element_type=jnp.float32)
    rest = jnp.dot(rest_left, rest_right, preferred_element_type=jnp.float32)
    return main[:, :width] + (main[:, width:] + rest)


def cell_roots(index, weight, cells):
    low = jnp.bitwise_and(index, LANES - 1)
    high = lax.shift_right_logical(index, LANES.bit_length() - 1)
    groups = cells // LANES
    obs = index.shape[1]
    square = weight * weight
    coarse = square.astype(jnp.bfloat16).astype(jnp.float32)
    in_group = lax.broadcasted_iota(jnp.int32, (groups, obs), 0) == high
    left = jnp.concatenate(
        [jnp.where(in_group, coarse, 0.0), jnp.where(in_group, square - coarse, 0.0)], axis=0
    ).astype(jnp.bfloat16)
    right = (lax.broadcasted_iota(jnp.int32, (LANES, obs), 0) == low)
    right = right.astype(jnp.float32).astype(jnp.bfloat16)
    both = lax.dot_general(
        left, right, (((1,), (1,)), ((), ())), preferred_element_type=jnp.float32
    )
    return jnp.sqrt(both[:groups] + both[groups:])


def gram_of(cells_at, roots):
    groups = roots.shape[0]
    scaled = jnp.concatenate(
        [
            (cells_at[:, g * LANES:(g + 1) * LANES].astype(jnp.float32) * roots[g:g + 1])
            .astype(jnp.bfloat16)
            for g in range(groups)
        ],
        axis=1,
    )
    return lax.dot_general(
        scaled, scaled, (((1,), (1,)), ((), ())), preferred_element_type=jnp.float32
    )


def inverse_of(matrix, identity, steps):
    size = matrix.shape[0]
    norm = jnp.max(jnp.sum(jnp.abs(matrix), axis=0, keepdims=True), axis=1, keepdims=True)
    least = jnp.broadcast_to(1.0 / norm, (1, size))
    own = matrix * least
    result = identity * least
    for step in range(steps):
        alpha = 2.0 / (1.0 + least)
        factor = (2.0 * alpha) * identity - (alpha * alpha) * own
        dot = exact_dot if step < steps - 5 else near_dot
        if step == 0:
            result = factor * least
            own = dot(own, factor)
        elif step == steps - 1:
            result = dot(result, factor)
        else:
            both = dot(jnp.concatenate([own, result], axis=0), factor)
            own, result = both[:size], both[size:]
        least = (alpha * alpha) * least
    return result


def tree(items):
    while len(items) > 1:
        paired = [near_dot(a, b) for a, b in zip(items[::2], items[1::2])]
        items = paired + items[len(items) - len(items) % 2:]
    return items[0]


def chain_kernel(space, tm, times, steps, anomalies_ref, index_ref, weight_ref, out_ref,
                 cells, index, weight, gram, near, joint, far, partner, matrix, weights, products, chains_ref,
                 load_sem, index_sem, weight_sem,
                 near_send, near_recv, far_send, far_recv, partner_send, partner_recv, share_send, share_recv,
                 spread_send, spread_recv, pass_send, pass_recv, time_send, time_recv,
                 relay_send, relay_recv):
    members = matrix.shape[0]
    me = lax.axis_index("space")
    mine = lax.axis_index("tm")
    rows = times * members // space
    team = space // times
    owned = me // team
    place = me % team
    base = owned * team

    def row_slice(number):
        return pl.ds(pl.multiple_of(number * rows, rows), rows)

    def to(source, target, send, recv, **device):
        return pltpu.make_async_remote_copy(
            src_ref=source, dst_ref=target, send_sem=send, recv_sem=recv,
            device_id=device, device_id_type=MESH,
        )

    order = [(owned + 1 + i) % times for i in range(times)]
    index_load = pltpu.make_async_copy(index_ref, index, index_sem)
    weight_load = pltpu.make_async_copy(weight_ref, weight, weight_sem)
    loads = [
        pltpu.make_async_copy(anomalies_ref.at[slot], cells.at[i], load_sem.at[i])
        for i, slot in enumerate(order)
    ]
    index_load.start()
    loads[0].start()
    weight_load.start()
    for load in loads[1:]:
        load.start()

    barrier = pltpu.get_barrier_semaphore()
    for d in range(1, space):
        pl.semaphore_signal(barrier, inc=1, device_id={"space": (me + d) % space}, device_id_type=MESH)
    for d in range(1, tm):
        pl.semaphore_signal(barrier, inc=1, device_id={"tm": (mine + d) % tm}, device_id_type=MESH)
    index_load.wait()
    weight_load.wait()

    sends = []
    near_copies = []
    far_copies = []

    def pass_on(i):
        piece = gram[order[i], row_slice(place), :]
        for copy in near_copies[i]:
            copy.wait_recv()
        for e in range(1, team):
            piece = piece + near[i, e]
        joint[i] = piece
        copy = to(joint.at[i], far.at[i], far_send.at[i], far_recv.at[i],
                  space=order[i] * team + place)
        copy.start()
        far_copies.append(copy)

    roots = [
        cell_roots(index[pl.ds(slot, 1), :], weight[pl.ds(slot, 1), :], cells.shape[2])
        for slot in order
    ]
    for i, slot in enumerate(order):
        loads[i].wait()
        gram[slot] = gram_of(cells.at[i], roots[i])
        if i == 0:
            pl.semaphore_wait(barrier, space + tm - 2)
        if i < times - 1:
            near_copies.append([])
            for e in range(1, team):
                peer = (place + e) % team
                copy = to(gram.at[slot, row_slice(peer)], near.at[i, e], near_send.at[i, e],
                          near_recv.at[i, e], space=base + peer)
                copy.start()
                near_copies[i].append(copy)
        if 2 <= i < times - 1:
            pass_on(i - 2)
    partners = []
    for e in range(1, team):
        copy = to(gram.at[owned], partner.at[e], partner_send.at[e], partner_recv.at[e],
                  space=base + (place + e) % team)
        copy.start()
        partners.append(copy)
    for i in range(max(times - 3, 0), times - 1):
        pass_on(i)
    for copy in far_copies:
        copy.wait_recv()
    matrix[row_slice(place), :] = jnp.sum(far[...], axis=0)
    shares = []
    for e in range(1, team):
        copy = to(matrix.at[row_slice(place)], matrix.at[row_slice(place)], share_send.at[e],
                  share_recv.at[e], space=base + (place + e) % team)
        copy.start()
        shares.append(copy)
    total = gram[owned]
    for copy in partners:
        copy.wait_recv()
    for e in range(1, team):
        total = total + partner[e]
    for e in range(1, team):
        origin = (place + team - e) % team
        to(matrix.at[row_slice(origin)], matrix.at[row_slice(origin)], share_send.at[e],
           share_recv.at[e], space=base + origin).wait_recv()
    total = total + matrix[...]

    identity = (
        lax.broadcasted_iota(jnp.int32, (members, members), 0)
        == lax.broadcasted_iota(jnp.int32, (members, members), 1)
    ).astype(jnp.float32)
    spread = float(members - 1)
    weights[owned] = inverse_of(identity + total / spread, identity, steps)

    def own_rows(slot):
        return weights.at[slot, row_slice(place)]

    for d in range(1, times):
        copy = to(own_rows(owned), own_rows(owned), spread_send.at[d], spread_recv.at[d],
                  space=((owned + d) % times) * team + place)
        copy.start()
        sends.append(copy)
    for d in range(1, times):
        slot = (owned + times - d) % times
        to(own_rows(slot), own_rows(slot), spread_send.at[d], spread_recv.at[d],
           space=slot * team + place).wait_recv()
        for e in range(1, team):
            copy = to(own_rows(slot), own_rows(slot), pass_send.at[d, e], pass_recv.at[d, e],
                      space=base + (place + e) % team)
            copy.start()
            sends.append(copy)
    for d in range(1, times):
        slot = (owned + times - d) % times
        for e in range(1, team):
            origin = (place + team - e) % team
            there = weights.at[slot, row_slice(origin)]
            to(there, there, pass_send.at[d, e], pass_recv.at[d, e], space=base + origin).wait_recv()

    each = [weights[t] for t in range(times)]
    products[mine] = tree(each)

    def product_rows(slot, number):
        return products.at[slot, row_slice(number)]

    for d in range(1, tm):
        @pl.when(mine >= d)
        def _(d=d):
            to(product_rows(mine, place), product_rows(mine, place), time_send.at[d],
               time_recv.at[d], tm=jnp.maximum(mine - d, 0)).start()

    tails = [identity]
    for t in range(times - 1, 0, -1):
        tails.append(near_dot(each[t], tails[-1]) if t < times - 1 else each[t])
    tails = tails[::-1]

    for d in range(1, tm):
        @pl.when(mine + d < tm)
        def _(d=d):
            slot = jnp.minimum(mine + d, tm - 1)
            to(product_rows(slot, place), product_rows(slot, place), time_send.at[d],
               time_recv.at[d], tm=slot).wait_recv()
            for e in range(1, team):
                to(product_rows(slot, place), product_rows(slot, place), relay_send.at[d, e],
                   relay_recv.at[d, e], space=base + (place + e) % team).start()
    chains_ref[...] = jnp.concatenate(tails, axis=0)
    for d in range(1, tm):
        @pl.when(mine + d < tm)
        def _(d=d):
            slot = jnp.minimum(mine + d, tm - 1)
            for e in range(1, team):
                origin = (place + team - e) % team
                to(product_rows(slot, origin), product_rows(slot, origin), relay_send.at[d, e],
                   relay_recv.at[d, e], space=base + origin).wait_recv()
            chains_ref[...] = near_dot(chains_ref[...], products[slot])

    for t in range(times):
        out_ref[t] = chains_ref[t * members:(t + 1) * members].T.astype(out_ref.dtype)

    for copy in sum(near_copies, sends + shares + partners + far_copies):
        copy.wait_send()
    for d in range(1, tm):
        @pl.when(mine >= d)
        def _(d=d):
            to(product_rows(mine, place), product_rows(mine, place), time_send.at[d],
               time_recv.at[d], tm=jnp.maximum(mine - d, 0)).wait_send()

        @pl.when(mine + d < tm)
        def _(d=d):
            slot = jnp.minimum(mine + d, tm - 1)
            for e in range(1, team):
                to(product_rows(slot, place), product_rows(slot, place), relay_send.at[d, e],
                   relay_recv.at[d, e], space=base + (place + e) % team).wait_send()


def smooth_kernel(chain_ref, anomalies_ref, out_ref, done, done_sem):
    times, members, cells = anomalies_ref.shape
    parts = done_sem.shape[1]
    width = cells // parts
    copies = []
    for t in range(times):
        for c in range(parts):
            part = slice(c * width, (c + 1) * width)
            done[t, :, part] = jnp.dot(
                chain_ref[t], anomalies_ref[t, :, part], preferred_element_type=jnp.float32
            ).astype(done.dtype)
            copy = pltpu.make_async_copy(
                done.at[t, :, part], out_ref.at[t, :, part], done_sem.at[t, c]
            )
            copy.start()
            copies.append(copy)
    for copy in copies:
        copy.wait()


def per_device(space, tm, anomalies, obs_index, obs_weight):
    times, members, cells = anomalies.shape
    obs = obs_index.shape[1]
    whole_vmem = pl.BlockSpec(memory_space=pltpu.VMEM)

    bound = 1.0 + members * obs * space * LARGEST_SCALED**2 / (members - 1)
    steps = math.ceil(math.log(bound / 4.0, 4)) + 3
    rows = times * members // space
    team = space // times
    dma = pltpu.SemaphoreType.DMA
    in_hbm = pl.BlockSpec(memory_space=pltpu.HBM)
    wide = jnp.float32
    square_wide = (members, members)
    chains = pl.pallas_call(
        functools.partial(chain_kernel, space, tm, times, steps),
        in_specs=[in_hbm] * 3,
        out_specs=whole_vmem,
        out_shape=jax.ShapeDtypeStruct((times, members, members), jnp.bfloat16),
        scratch_shapes=[
            pltpu.VMEM(anomalies.shape, anomalies.dtype),
            pltpu.VMEM(obs_index.shape, obs_index.dtype),
            pltpu.VMEM(obs_weight.shape, obs_weight.dtype),
            pltpu.VMEM((times, *square_wide), wide),
            pltpu.VMEM((times - 1, team, rows, members), wide),
            pltpu.VMEM((times - 1, rows, members), wide),
            pltpu.VMEM((times - 1, rows, members), wide),
            pltpu.VMEM((team, *square_wide), wide),
            pltpu.VMEM(square_wide, wide),
            pltpu.VMEM((times, *square_wide), wide),
            pltpu.VMEM((tm, *square_wide), wide),
            pltpu.VMEM((times * members, members), wide),
            dma((times,)), dma, dma,
            dma((times, team)), dma((times, team)), dma((times,)), dma((times,)), dma((team,)), dma((team,)),
            dma((team,)), dma((team,)), dma((times,)), dma((times,)),
            dma((times, team)), dma((times, team)), dma((tm,)), dma((tm,)),
            dma((tm, team)), dma((tm, team)),
        ],
        compiler_params=pltpu.CompilerParams(
            collective_id=0, has_side_effects=True, vmem_limit_bytes=40 * 2**20
        ),
    )(*(pltpu.with_memory_space_constraint(x, pltpu.HBM) for x in (anomalies, obs_index, obs_weight)))

    return pl.pallas_call(
        smooth_kernel,
        in_specs=[whole_vmem, whole_vmem],
        out_specs=in_hbm,
        out_shape=jax.ShapeDtypeStruct(anomalies.shape, anomalies.dtype),
        scratch_shapes=[pltpu.VMEM(anomalies.shape, anomalies.dtype), dma((times, 2))],
        compiler_params=pltpu.CompilerParams(vmem_limit_bytes=40 * 2**20),
    )(chains, anomalies)


def solution(mesh):
    return jax.shard_map(
        functools.partial(per_device, mesh.shape["space"], mesh.shape["tm"]),
        mesh=mesh,
        in_specs=(P("tm", None, "space"), P("tm", "space"), P("tm", "space")),
        out_specs=P("tm", None, "space"),
        check_vma=False,
    )
```

```python
import functools
import math

import jax
import jax.numpy as jnp
from jax import lax
from jax.experimental import pallas as pl
from jax.experimental.pallas import tpu as pltpu
from jax.sharding import PartitionSpec as P

MESH = pl.DeviceIdType.MESH
LANES = 128
LARGEST_SCALED = 51.0 * 0.12


def split(value):
    high = value.astype(jnp.bfloat16)
    rest = value - high.astype(jnp.float32)
    return high, rest.astype(jnp.bfloat16), rest


def near_dot(left, right):
    width = right.shape[1]
    left_high, left_middle, _ = split(left)
    right_high, right_middle, _ = split(right)
    main_left = jnp.concatenate([left_high, left_middle], axis=1)
    main_row = jnp.concatenate([right_high, right_middle], axis=1)
    main_right = jnp.concatenate([main_row, main_row], axis=0)
    main = jnp.dot(main_left, main_right, preferred_element_type=jnp.float32)
    return main[:, :width] + main[:, width:]


def exact_dot(left, right):
    width = right.shape[1]
    left_high, left_middle, left_rest = split(left)
    right_high, right_middle, right_rest = split(right)
    left_low = (left_rest - left_middle.astype(jnp.float32)).astype(jnp.bfloat16)
    right_low = (right_rest - right_middle.astype(jnp.float32)).astype(jnp.bfloat16)
    main_left = jnp.concatenate([left_high, left_middle], axis=1)
    main_row = jnp.concatenate([right_high, right_middle], axis=1)
    main_right = jnp.concatenate([main_row, main_row], axis=0)
    rest_left = jnp.concatenate([left_high, left_low], axis=1)
    rest_right = jnp.concatenate([right_low, right_high], axis=0)
    main = jnp.dot(main_left, main_right, preferred_element_type=jnp.float32)
    rest = jnp.dot(rest_left, rest_right, preferred_element_type=jnp.float32)
    return main[:, :width] + (main[:, width:] + rest)


def cell_roots(index, weight, cells):
    low = jnp.bitwise_and(index, LANES - 1)
    high = lax.shift_right_logical(index, LANES.bit_length() - 1)
    groups = cells // LANES
    obs = index.shape[1]
    square = weight * weight
    coarse = square.astype(jnp.bfloat16).astype(jnp.float32)
    in_group = lax.broadcasted_iota(jnp.int32, (groups, obs), 0) == high
    left = jnp.concatenate(
        [jnp.where(in_group, coarse, 0.0), jnp.where(in_group, square - coarse, 0.0)], axis=0
    ).astype(jnp.bfloat16)
    right = (lax.broadcasted_iota(jnp.int32, (LANES, obs), 0) == low)
    right = right.astype(jnp.float32).astype(jnp.bfloat16)
    both = lax.dot_general(
        left, right, (((1,), (1,)), ((), ())), preferred_element_type=jnp.float32
    )
    return jnp.sqrt(both[:groups] + both[groups:])


def gram_of(cells_at, roots):
    groups = roots.shape[0]
    scaled = jnp.concatenate(
        [
            (cells_at[:, g * LANES:(g + 1) * LANES].astype(jnp.float32) * roots[g:g + 1])
            .astype(jnp.bfloat16)
            for g in range(groups)
        ],
        axis=1,
    )
    return lax.dot_general(
        scaled, scaled, (((1,), (1,)), ((), ())), preferred_element_type=jnp.float32
    )


def inverse_of(matrix, identity, steps):
    size = matrix.shape[0]
    norm = jnp.max(jnp.sum(jnp.abs(matrix), axis=0, keepdims=True), axis=1, keepdims=True)
    least = jnp.broadcast_to(1.0 / norm, (1, size))
    own = matrix * least
    result = identity * least
    for step in range(steps):
        alpha = 2.0 / (1.0 + least)
        factor = (2.0 * alpha) * identity - (alpha * alpha) * own
        dot = exact_dot if step < steps - 5 else near_dot
        if step == 0:
            result = factor * least
            own = dot(own, factor)
        elif step == steps - 1:
            result = dot(result, factor)
        else:
            both = dot(jnp.concatenate([own, result], axis=0), factor)
            own, result = both[:size], both[size:]
        least = (alpha * alpha) * least
    return result


def tree(items):
    while len(items) > 1:
        paired = [near_dot(a, b) for a, b in zip(items[::2], items[1::2])]
        items = paired + items[len(items) - len(items) % 2:]
    return items[0]


def chain_kernel(space, tm, times, steps, anomalies_ref, index_ref, weight_ref, out_ref,
                 cells, index, weight, gram, near, joint, far, partner, matrix, weights, products, chains_ref,
                 load_sem, index_sem, weight_sem,
                 near_send, near_recv, far_send, far_recv, partner_send, partner_recv, share_send, share_recv,
                 spread_send, spread_recv, pass_send, pass_recv, time_send, time_recv):
    members = matrix.shape[0]
    me = lax.axis_index("space")
    mine = lax.axis_index("tm")
    rows = times * members // space
    team = space // times
    owned = me // team
    place = me % team
    base = owned * team

    def row_slice(number):
        return pl.ds(pl.multiple_of(number * rows, rows), rows)

    def to(source, target, send, recv, **device):
        return pltpu.make_async_remote_copy(
            src_ref=source, dst_ref=target, send_sem=send, recv_sem=recv,
            device_id=device, device_id_type=MESH,
        )

    order = [(owned + 1 + i) % times for i in range(times)]
    index_load = pltpu.make_async_copy(index_ref, index, index_sem)
    weight_load = pltpu.make_async_copy(weight_ref, weight, weight_sem)
    loads = [
        pltpu.make_async_copy(anomalies_ref.at[slot], cells.at[i], load_sem.at[i])
        for i, slot in enumerate(order)
    ]
    index_load.start()
    loads[0].start()
    weight_load.start()
    for load in loads[1:]:
        load.start()

    barrier = pltpu.get_barrier_semaphore()
    for d in range(1, space):
        pl.semaphore_signal(barrier, inc=1, device_id={"space": (me + d) % space}, device_id_type=MESH)
    for d in range(1, tm):
        pl.semaphore_signal(barrier, inc=1, device_id={"tm": (mine + d) % tm}, device_id_type=MESH)
    index_load.wait()
    weight_load.wait()

    sends = []
    near_copies = []
    far_copies = []

    def pass_on(i):
        piece = gram[order[i], row_slice(place), :]
        for copy in near_copies[i]:
            copy.wait_recv()
        for e in range(1, team):
            piece = piece + near[i, e]
        joint[i] = piece
        copy = to(joint.at[i], far.at[i], far_send.at[i], far_recv.at[i],
                  space=order[i] * team + place)
        copy.start()
        far_copies.append(copy)

    roots = [
        cell_roots(index[pl.ds(slot, 1), :], weight[pl.ds(slot, 1), :], cells.shape[2])
        for slot in order
    ]
    for i, slot in enumerate(order):
        loads[i].wait()
        gram[slot] = gram_of(cells.at[i], roots[i])
        if i == 0:
            pl.semaphore_wait(barrier, space + tm - 2)
        if i < times - 1:
            near_copies.append([])
            for e in range(1, team):
                peer = (place + e) % team
                copy = to(gram.at[slot, row_slice(peer)], near.at[i, e], near_send.at[i, e],
                          near_recv.at[i, e], space=base + peer)
                copy.start()
                near_copies[i].append(copy)
        if 2 <= i < times - 1:
            pass_on(i - 2)
    partners = []
    for e in range(1, team):
        copy = to(gram.at[owned], partner.at[e], partner_send.at[e], partner_recv.at[e],
                  space=base + (place + e) % team)
        copy.start()
        partners.append(copy)
    for i in range(max(times - 3, 0), times - 1):
        pass_on(i)
    for copy in far_copies:
        copy.wait_recv()
    matrix[row_slice(place), :] = jnp.sum(far[...], axis=0)
    shares = []
    for e in range(1, team):
        copy = to(matrix.at[row_slice(place)], matrix.at[row_slice(place)], share_send.at[e],
                  share_recv.at[e], space=base + (place + e) % team)
        copy.start()
        shares.append(copy)
    total = gram[owned]
    for copy in partners:
        copy.wait_recv()
    for e in range(1, team):
        total = total + partner[e]
    for e in range(1, team):
        origin = (place + team - e) % team
        to(matrix.at[row_slice(origin)], matrix.at[row_slice(origin)], share_send.at[e],
           share_recv.at[e], space=base + origin).wait_recv()
    total = total + matrix[...]

    identity = (
        lax.broadcasted_iota(jnp.int32, (members, members), 0)
        == lax.broadcasted_iota(jnp.int32, (members, members), 1)
    ).astype(jnp.float32)
    spread = float(members - 1)
    weights[owned] = inverse_of(identity + total / spread, identity, steps)

    def own_rows(slot):
        return weights.at[slot, row_slice(place)]

    for d in range(1, times):
        copy = to(own_rows(owned), own_rows(owned), spread_send.at[d], spread_recv.at[d],
                  space=((owned + d) % times) * team + place)
        copy.start()
        sends.append(copy)
    for d in range(1, times):
        slot = (owned + times - d) % times
        to(own_rows(slot), own_rows(slot), spread_send.at[d], spread_recv.at[d],
           space=slot * team + place).wait_recv()
        for e in range(1, team):
            copy = to(own_rows(slot), own_rows(slot), pass_send.at[d, e], pass_recv.at[d, e],
                      space=base + (place + e) % team)
            copy.start()
            sends.append(copy)
    for d in range(1, times):
        slot = (owned + times - d) % times
        for e in range(1, team):
            origin = (place + team - e) % team
            there = weights.at[slot, row_slice(origin)]
            to(there, there, pass_send.at[d, e], pass_recv.at[d, e], space=base + origin).wait_recv()

    each = [weights[t] for t in range(times)]
    products[mine] = tree(each)

    for d in range(1, tm):
        @pl.when(mine >= d)
        def _(d=d):
            to(products.at[mine], products.at[mine], time_send.at[d], time_recv.at[d],
               tm=jnp.maximum(mine - d, 0)).start()

    tails = [identity]
    for t in range(times - 1, 0, -1):
        tails.append(near_dot(each[t], tails[-1]) if t < times - 1 else each[t])
    tails = tails[::-1]

    chains_ref[...] = jnp.concatenate(tails, axis=0)
    for d in range(1, tm):
        @pl.when(mine + d < tm)
        def _(d=d):
            slot = jnp.minimum(mine + d, tm - 1)
            to(products.at[slot], products.at[slot], time_send.at[d], time_recv.at[d],
               tm=slot).wait_recv()
            chains_ref[...] = near_dot(chains_ref[...], products[slot])

    for t in range(times):
        out_ref[t] = chains_ref[t * members:(t + 1) * members].T.astype(out_ref.dtype)

    for copy in sum(near_copies, sends + shares + partners + far_copies):
        copy.wait_send()
    for d in range(1, tm):
        @pl.when(mine >= d)
        def _(d=d):
            to(products.at[mine], products.at[mine], time_send.at[d], time_recv.at[d],
               tm=jnp.maximum(mine - d, 0)).wait_send()


def smooth_kernel(chain_ref, anomalies_ref, out_ref, done, done_sem):
    times, members, cells = anomalies_ref.shape
    parts = done_sem.shape[1]
    width = cells // parts
    copies = []
    for t in range(times):
        for c in range(parts):
            part = slice(c * width, (c + 1) * width)
            done[t, :, part] = jnp.dot(
                chain_ref[t], anomalies_ref[t, :, part], preferred_element_type=jnp.float32
            ).astype(done.dtype)
            copy = pltpu.make_async_copy(
                done.at[t, :, part], out_ref.at[t, :, part], done_sem.at[t, c]
            )
            copy.start()
            copies.append(copy)
    for copy in copies:
        copy.wait()


def per_device(space, tm, anomalies, obs_index, obs_weight):
    times, members, cells = anomalies.shape
    obs = obs_index.shape[1]
    whole_vmem = pl.BlockSpec(memory_space=pltpu.VMEM)

    bound = 1.0 + members * obs * space * LARGEST_SCALED**2 / (members - 1)
    steps = math.ceil(math.log(bound / 4.0, 4)) + 3
    rows = times * members // space
    team = space // times
    dma = pltpu.SemaphoreType.DMA
    in_hbm = pl.BlockSpec(memory_space=pltpu.HBM)
    wide = jnp.float32
    square_wide = (members, members)
    chains = pl.pallas_call(
        functools.partial(chain_kernel, space, tm, times, steps),
        in_specs=[in_hbm] * 3,
        out_specs=whole_vmem,
        out_shape=jax.ShapeDtypeStruct((times, members, members), jnp.bfloat16),
        scratch_shapes=[
            pltpu.VMEM(anomalies.shape, anomalies.dtype),
            pltpu.VMEM(obs_index.shape, obs_index.dtype),
            pltpu.VMEM(obs_weight.shape, obs_weight.dtype),
            pltpu.VMEM((times, *square_wide), wide),
            pltpu.VMEM((times - 1, team, rows, members), wide),
            pltpu.VMEM((times - 1, rows, members), wide),
            pltpu.VMEM((times - 1, rows, members), wide),
            pltpu.VMEM((team, *square_wide), wide),
            pltpu.VMEM(square_wide, wide),
            pltpu.VMEM((times, *square_wide), wide),
            pltpu.VMEM((tm, *square_wide), wide),
            pltpu.VMEM((times * members, members), wide),
            dma((times,)), dma, dma,
            dma((times, team)), dma((times, team)), dma((times,)), dma((times,)), dma((team,)), dma((team,)),
            dma((team,)), dma((team,)), dma((times,)), dma((times,)),
            dma((times, team)), dma((times, team)), dma((tm,)), dma((tm,)),
        ],
        compiler_params=pltpu.CompilerParams(
            collective_id=0, has_side_effects=True, vmem_limit_bytes=40 * 2**20
        ),
    )(*(pltpu.with_memory_space_constraint(x, pltpu.HBM) for x in (anomalies, obs_index, obs_weight)))

    return pl.pallas_call(
        smooth_kernel,
        in_specs=[whole_vmem, whole_vmem],
        out_specs=in_hbm,
        out_shape=jax.ShapeDtypeStruct(anomalies.shape, anomalies.dtype),
        scratch_shapes=[pltpu.VMEM(anomalies.shape, anomalies.dtype), dma((times, 2))],
        compiler_params=pltpu.CompilerParams(vmem_limit_bytes=40 * 2**20),
    )(chains, anomalies)


def solution(mesh):
    return jax.shard_map(
        functools.partial(per_device, mesh.shape["space"], mesh.shape["tm"]),
        mesh=mesh,
        in_specs=(P("tm", None, "space"), P("tm", "space"), P("tm", "space")),
        out_specs=P("tm", None, "space"),
        check_vma=False,
    )
```

```python
import functools
import math

import jax
import jax.numpy as jnp
from jax import lax
from jax.experimental import pallas as pl
from jax.experimental.pallas import tpu as pltpu
from jax.sharding import PartitionSpec as P

MESH = pl.DeviceIdType.MESH
LANES = 128
LARGEST_SCALED = 51.0 * 0.12


def split(value):
    high = value.astype(jnp.bfloat16)
    rest = value - high.astype(jnp.float32)
    return high, rest.astype(jnp.bfloat16), rest


def near_dot(left, right):
    width = right.shape[1]
    left_high, left_middle, _ = split(left)
    right_high, right_middle, _ = split(right)
    main_left = jnp.concatenate([left_high, left_middle], axis=1)
    main_row = jnp.concatenate([right_high, right_middle], axis=1)
    main_right = jnp.concatenate([main_row, main_row], axis=0)
    main = jnp.dot(main_left, main_right, preferred_element_type=jnp.float32)
    return main[:, :width] + main[:, width:]


def exact_dot(left, right):
    width = right.shape[1]
    left_high, left_middle, left_rest = split(left)
    right_high, right_middle, right_rest = split(right)
    left_low = (left_rest - left_middle.astype(jnp.float32)).astype(jnp.bfloat16)
    right_low = (right_rest - right_middle.astype(jnp.float32)).astype(jnp.bfloat16)
    main_left = jnp.concatenate([left_high, left_middle], axis=1)
    main_row = jnp.concatenate([right_high, right_middle], axis=1)
    main_right = jnp.concatenate([main_row, main_row], axis=0)
    rest_left = jnp.concatenate([left_high, left_low], axis=1)
    rest_right = jnp.concatenate([right_low, right_high], axis=0)
    main = jnp.dot(main_left, main_right, preferred_element_type=jnp.float32)
    rest = jnp.dot(rest_left, rest_right, preferred_element_type=jnp.float32)
    return main[:, :width] + (main[:, width:] + rest)


def cell_roots(index, weight, cells):
    low = jnp.bitwise_and(index, LANES - 1)
    high = lax.shift_right_logical(index, LANES.bit_length() - 1)
    groups = cells // LANES
    obs = index.shape[1]
    square = weight * weight
    coarse = square.astype(jnp.bfloat16).astype(jnp.float32)
    in_group = lax.broadcasted_iota(jnp.int32, (groups, obs), 0) == high
    left = jnp.concatenate(
        [jnp.where(in_group, coarse, 0.0), jnp.where(in_group, square - coarse, 0.0)], axis=0
    ).astype(jnp.bfloat16)
    right = (lax.broadcasted_iota(jnp.int32, (LANES, obs), 0) == low)
    right = right.astype(jnp.float32).astype(jnp.bfloat16)
    both = lax.dot_general(
        left, right, (((1,), (1,)), ((), ())), preferred_element_type=jnp.float32
    )
    return jnp.sqrt(both[:groups] + both[groups:])


def gram_of(cells_at, roots):
    groups = roots.shape[0]
    scaled = jnp.concatenate(
        [
            (cells_at[:, g * LANES:(g + 1) * LANES].astype(jnp.float32) * roots[g:g + 1])
            .astype(jnp.bfloat16)
            for g in range(groups)
        ],
        axis=1,
    )
    return lax.dot_general(
        scaled, scaled, (((1,), (1,)), ((), ())), preferred_element_type=jnp.float32
    )


def inverse_of(matrix, identity, steps):
    size = matrix.shape[0]
    norm = jnp.max(jnp.sum(jnp.abs(matrix), axis=0, keepdims=True), axis=1, keepdims=True)
    least = jnp.broadcast_to(1.0 / norm, (1, size))
    own = matrix * least
    result = identity * least
    for step in range(steps):
        alpha = 2.0 / (1.0 + least)
        factor = (2.0 * alpha) * identity - (alpha * alpha) * own
        dot = exact_dot if step < steps - 7 else near_dot
        if step == 0:
            result = factor * least
            own = dot(own, factor)
        elif step == steps - 1:
            result = dot(result, factor)
        else:
            both = dot(jnp.concatenate([own, result], axis=0), factor)
            own, result = both[:size], both[size:]
        least = (alpha * alpha) * least
    return result


def tree(items):
    while len(items) > 1:
        paired = [near_dot(a, b) for a, b in zip(items[::2], items[1::2])]
        items = paired + items[len(items) - len(items) % 2:]
    return items[0]


def chain_kernel(space, tm, times, steps, anomalies_ref, index_ref, weight_ref, out_ref,
                 cells, index, weight, gram, near, joint, far, partner, matrix, weights, products, chains_ref,
                 load_sem, index_sem, weight_sem,
                 near_send, near_recv, far_send, far_recv, partner_send, partner_recv, share_send, share_recv,
                 spread_send, spread_recv, pass_send, pass_recv, time_send, time_recv,
                 relay_send, relay_recv):
    members = matrix.shape[0]
    me = lax.axis_index("space")
    mine = lax.axis_index("tm")
    rows = times * members // space
    team = space // times
    owned = me // team
    place = me % team
    base = owned * team

    def row_slice(number):
        return pl.ds(pl.multiple_of(number * rows, rows), rows)

    def to(source, target, send, recv, **device):
        return pltpu.make_async_remote_copy(
            src_ref=source, dst_ref=target, send_sem=send, recv_sem=recv,
            device_id=device, device_id_type=MESH,
        )

    order = [(owned + 1 + i) % times for i in range(times)]
    index_load = pltpu.make_async_copy(index_ref, index, index_sem)
    weight_load = pltpu.make_async_copy(weight_ref, weight, weight_sem)
    loads = [
        pltpu.make_async_copy(anomalies_ref.at[slot], cells.at[i], load_sem.at[i])
        for i, slot in enumerate(order)
    ]
    index_load.start()
    loads[0].start()
    weight_load.start()
    for load in loads[1:]:
        load.start()

    barrier = pltpu.get_barrier_semaphore()
    for d in range(1, space):
        pl.semaphore_signal(barrier, inc=1, device_id={"space": (me + d) % space}, device_id_type=MESH)
    for d in range(1, tm):
        pl.semaphore_signal(barrier, inc=1, device_id={"tm": (mine + d) % tm}, device_id_type=MESH)
    index_load.wait()
    weight_load.wait()

    sends = []
    near_copies = []
    far_copies = []

    def pass_on(i):
        piece = gram[order[i], row_slice(place), :]
        for copy in near_copies[i]:
            copy.wait_recv()
        for e in range(1, team):
            piece = piece + near[i, e]
        joint[i] = piece
        copy = to(joint.at[i], far.at[i], far_send.at[i], far_recv.at[i],
                  space=order[i] * team + place)
        copy.start()
        far_copies.append(copy)

    roots = [
        cell_roots(index[pl.ds(slot, 1), :], weight[pl.ds(slot, 1), :], cells.shape[2])
        for slot in order
    ]
    for i, slot in enumerate(order):
        loads[i].wait()
        gram[slot] = gram_of(cells.at[i], roots[i])
        if i == 0:
            pl.semaphore_wait(barrier, space + tm - 2)
        if i < times - 1:
            near_copies.append([])
            for e in range(1, team):
                peer = (place + e) % team
                copy = to(gram.at[slot, row_slice(peer)], near.at[i, e], near_send.at[i, e],
                          near_recv.at[i, e], space=base + peer)
                copy.start()
                near_copies[i].append(copy)
        if 2 <= i < times - 1:
            pass_on(i - 2)
    partners = []
    for e in range(1, team):
        copy = to(gram.at[owned], partner.at[e], partner_send.at[e], partner_recv.at[e],
                  space=base + (place + e) % team)
        copy.start()
        partners.append(copy)
    for i in range(max(times - 3, 0), times - 1):
        pass_on(i)
    for copy in far_copies:
        copy.wait_recv()
    matrix[row_slice(place), :] = jnp.sum(far[...], axis=0)
    shares = []
    for e in range(1, team):
        copy = to(matrix.at[row_slice(place)], matrix.at[row_slice(place)], share_send.at[e],
                  share_recv.at[e], space=base + (place + e) % team)
        copy.start()
        shares.append(copy)
    total = gram[owned]
    for copy in partners:
        copy.wait_recv()
    for e in range(1, team):
        total = total + partner[e]
    for e in range(1, team):
        origin = (place + team - e) % team
        to(matrix.at[row_slice(origin)], matrix.at[row_slice(origin)], share_send.at[e],
           share_recv.at[e], space=base + origin).wait_recv()
    total = total + matrix[...]

    identity = (
        lax.broadcasted_iota(jnp.int32, (members, members), 0)
        == lax.broadcasted_iota(jnp.int32, (members, members), 1)
    ).astype(jnp.float32)
    spread = float(members - 1)
    weights[owned] = inverse_of(identity + total / spread, identity, steps)

    def own_rows(slot):
        return weights.at[slot, row_slice(place)]

    for d in range(1, times):
        copy = to(own_rows(owned), own_rows(owned), spread_send.at[d], spread_recv.at[d],
                  space=((owned + d) % times) * team + place)
        copy.start()
        sends.append(copy)
    for d in range(1, times):
        slot = (owned + times - d) % times
        to(own_rows(slot), own_rows(slot), spread_send.at[d], spread_recv.at[d],
           space=slot * team + place).wait_recv()
        for e in range(1, team):
            copy = to(own_rows(slot), own_rows(slot), pass_send.at[d, e], pass_recv.at[d, e],
                      space=base + (place + e) % team)
            copy.start()
            sends.append(copy)
    for d in range(1, times):
        slot = (owned + times - d) % times
        for e in range(1, team):
            origin = (place + team - e) % team
            there = weights.at[slot, row_slice(origin)]
            to(there, there, pass_send.at[d, e], pass_recv.at[d, e], space=base + origin).wait_recv()

    each = [weights[t] for t in range(times)]
    products[mine] = tree(each)

    def product_rows(slot, number):
        return products.at[slot, row_slice(number)]

    for d in range(tm - 1, 0, -1):
        @pl.when(mine >= d)
        def _(d=d):
            to(product_rows(mine, place), product_rows(mine, place), time_send.at[d],
               time_recv.at[d], tm=jnp.maximum(mine - d, 0)).start()

    tails = [identity]
    for t in range(times - 1, 0, -1):
        tails.append(near_dot(each[t], tails[-1]) if t < times - 1 else each[t])
    tails = tails[::-1]

    for d in range(1, tm):
        @pl.when(mine + d < tm)
        def _(d=d):
            slot = jnp.minimum(mine + d, tm - 1)
            to(product_rows(slot, place), product_rows(slot, place), time_send.at[d],
               time_recv.at[d], tm=slot).wait_recv()
            for e in range(1, team):
                to(product_rows(slot, place), product_rows(slot, place), relay_send.at[d, e],
                   relay_recv.at[d, e], space=base + (place + e) % team).start()
    chains_ref[...] = jnp.concatenate(tails, axis=0)
    for d in range(1, tm):
        @pl.when(mine + d < tm)
        def _(d=d):
            slot = jnp.minimum(mine + d, tm - 1)
            for e in range(1, team):
                origin = (place + team - e) % team
                to(product_rows(slot, origin), product_rows(slot, origin), relay_send.at[d, e],
                   relay_recv.at[d, e], space=base + origin).wait_recv()
            chains_ref[...] = near_dot(chains_ref[...], products[slot])

    for t in range(times):
        out_ref[t] = chains_ref[t * members:(t + 1) * members].T.astype(out_ref.dtype)

    for copy in sum(near_copies, sends + shares + partners + far_copies):
        copy.wait_send()
    for d in range(1, tm):
        @pl.when(mine >= d)
        def _(d=d):
            to(product_rows(mine, place), product_rows(mine, place), time_send.at[d],
               time_recv.at[d], tm=jnp.maximum(mine - d, 0)).wait_send()

        @pl.when(mine + d < tm)
        def _(d=d):
            slot = jnp.minimum(mine + d, tm - 1)
            for e in range(1, team):
                to(product_rows(slot, place), product_rows(slot, place), relay_send.at[d, e],
                   relay_recv.at[d, e], space=base + (place + e) % team).wait_send()


def smooth_kernel(chain_ref, anomalies_ref, out_ref, done, done_sem):
    times, members, cells = anomalies_ref.shape
    parts = done_sem.shape[1]
    width = cells // parts
    copies = []
    for t in range(times):
        for c in range(parts):
            part = slice(c * width, (c + 1) * width)
            done[t, :, part] = jnp.dot(
                chain_ref[t], anomalies_ref[t, :, part], preferred_element_type=jnp.float32
            ).astype(done.dtype)
            copy = pltpu.make_async_copy(
                done.at[t, :, part], out_ref.at[t, :, part], done_sem.at[t, c]
            )
            copy.start()
            copies.append(copy)
    for copy in copies:
        copy.wait()


def per_device(space, tm, anomalies, obs_index, obs_weight):
    times, members, cells = anomalies.shape
    obs = obs_index.shape[1]
    whole_vmem = pl.BlockSpec(memory_space=pltpu.VMEM)

    bound = 1.0 + members * obs * space * LARGEST_SCALED**2 / (members - 1)
    steps = math.ceil(math.log(bound / 4.0, 4)) + 3
    rows = times * members // space
    team = space // times
    dma = pltpu.SemaphoreType.DMA
    in_hbm = pl.BlockSpec(memory_space=pltpu.HBM)
    wide = jnp.float32
    square_wide = (members, members)
    chains = pl.pallas_call(
        functools.partial(chain_kernel, space, tm, times, steps),
        in_specs=[in_hbm] * 3,
        out_specs=whole_vmem,
        out_shape=jax.ShapeDtypeStruct((times, members, members), jnp.bfloat16),
        scratch_shapes=[
            pltpu.VMEM(anomalies.shape, anomalies.dtype),
            pltpu.VMEM(obs_index.shape, obs_index.dtype),
            pltpu.VMEM(obs_weight.shape, obs_weight.dtype),
            pltpu.VMEM((times, *square_wide), wide),
            pltpu.VMEM((times - 1, team, rows, members), wide),
            pltpu.VMEM((times - 1, rows, members), wide),
            pltpu.VMEM((times - 1, rows, members), wide),
            pltpu.VMEM((team, *square_wide), wide),
            pltpu.VMEM(square_wide, wide),
            pltpu.VMEM((times, *square_wide), wide),
            pltpu.VMEM((tm, *square_wide), wide),
            pltpu.VMEM((times * members, members), wide),
            dma((times,)), dma, dma,
            dma((times, team)), dma((times, team)), dma((times,)), dma((times,)), dma((team,)), dma((team,)),
            dma((team,)), dma((team,)), dma((times,)), dma((times,)),
            dma((times, team)), dma((times, team)), dma((tm,)), dma((tm,)),
            dma((tm, team)), dma((tm, team)),
        ],
        compiler_params=pltpu.CompilerParams(
            collective_id=0, has_side_effects=True, vmem_limit_bytes=40 * 2**20
        ),
    )(*(pltpu.with_memory_space_constraint(x, pltpu.HBM) for x in (anomalies, obs_index, obs_weight)))

    return pl.pallas_call(
        smooth_kernel,
        in_specs=[whole_vmem, whole_vmem],
        out_specs=in_hbm,
        out_shape=jax.ShapeDtypeStruct(anomalies.shape, anomalies.dtype),
        scratch_shapes=[pltpu.VMEM(anomalies.shape, anomalies.dtype), dma((times, 2))],
        compiler_params=pltpu.CompilerParams(vmem_limit_bytes=40 * 2**20),
    )(chains, anomalies)


def solution(mesh):
    return jax.shard_map(
        functools.partial(per_device, mesh.shape["space"], mesh.shape["tm"]),
        mesh=mesh,
        in_specs=(P("tm", None, "space"), P("tm", "space"), P("tm", "space")),
        out_specs=P("tm", None, "space"),
        check_vma=False,
    )
```

```python
import functools
import math

import jax
import jax.numpy as jnp
from jax import lax
from jax.experimental import pallas as pl
from jax.experimental.pallas import tpu as pltpu
from jax.sharding import PartitionSpec as P

MESH = pl.DeviceIdType.MESH
LANES = 128
LARGEST_SCALED = 51.0 * 0.12


def split(value):
    high = value.astype(jnp.bfloat16)
    rest = value - high.astype(jnp.float32)
    return high, rest.astype(jnp.bfloat16), rest


def near_dot(left, right):
    width = right.shape[1]
    left_high, left_middle, _ = split(left)
    right_high, right_middle, _ = split(right)
    main_left = jnp.concatenate([left_high, left_middle], axis=1)
    main_row = jnp.concatenate([right_high, right_middle], axis=1)
    main_right = jnp.concatenate([main_row, main_row], axis=0)
    main = jnp.dot(main_left, main_right, preferred_element_type=jnp.float32)
    return main[:, :width] + main[:, width:]


def exact_dot(left, right):
    width = right.shape[1]
    left_high, left_middle, left_rest = split(left)
    right_high, right_middle, right_rest = split(right)
    left_low = (left_rest - left_middle.astype(jnp.float32)).astype(jnp.bfloat16)
    right_low = (right_rest - right_middle.astype(jnp.float32)).astype(jnp.bfloat16)
    main_left = jnp.concatenate([left_high, left_middle], axis=1)
    main_row = jnp.concatenate([right_high, right_middle], axis=1)
    main_right = jnp.concatenate([main_row, main_row], axis=0)
    rest_left = jnp.concatenate([left_high, left_low], axis=1)
    rest_right = jnp.concatenate([right_low, right_high], axis=0)
    main = jnp.dot(main_left, main_right, preferred_element_type=jnp.float32)
    rest = jnp.dot(rest_left, rest_right, preferred_element_type=jnp.float32)
    return main[:, :width] + (main[:, width:] + rest)


def cell_roots(index, weight, cells):
    low = jnp.bitwise_and(index, LANES - 1)
    high = lax.shift_right_logical(index, LANES.bit_length() - 1)
    groups = cells // LANES
    obs = index.shape[1]
    square = weight * weight
    coarse = square.astype(jnp.bfloat16).astype(jnp.float32)
    in_group = lax.broadcasted_iota(jnp.int32, (groups, obs), 0) == high
    left = jnp.concatenate(
        [jnp.where(in_group, coarse, 0.0), jnp.where(in_group, square - coarse, 0.0)], axis=0
    ).astype(jnp.bfloat16)
    right = (lax.broadcasted_iota(jnp.int32, (LANES, obs), 0) == low)
    right = right.astype(jnp.float32).astype(jnp.bfloat16)
    both = lax.dot_general(
        left, right, (((1,), (1,)), ((), ())), preferred_element_type=jnp.float32
    )
    return jnp.sqrt(both[:groups] + both[groups:])


def gram_of(cells_at, roots):
    groups = roots.shape[0]
    scaled = jnp.concatenate(
        [
            (cells_at[:, g * LANES:(g + 1) * LANES].astype(jnp.float32) * roots[g:g + 1])
            .astype(jnp.bfloat16)
            for g in range(groups)
        ],
        axis=1,
    )
    return lax.dot_general(
        scaled, scaled, (((1,), (1,)), ((), ())), preferred_element_type=jnp.float32
    )


def inverse_of(matrix, identity, steps):
    size = matrix.shape[0]
    norm = jnp.max(jnp.sum(jnp.abs(matrix), axis=0, keepdims=True), axis=1, keepdims=True)
    least = jnp.broadcast_to(1.0 / norm, (1, size))
    own = matrix * least
    result = identity * least
    for step in range(steps):
        alpha = 2.0 / (1.0 + least)
        factor = (2.0 * alpha) * identity - (alpha * alpha) * own
        dot = exact_dot if step < steps - 7 else near_dot
        if step == 0:
            result = factor * least
            own = dot(own, factor)
        elif step == steps - 1:
            result = dot(result, factor)
        else:
            both = dot(jnp.concatenate([own, result], axis=0), factor)
            own, result = both[:size], both[size:]
        least = (alpha * alpha) * least
    return result


def tree(items):
    while len(items) > 1:
        paired = [near_dot(a, b) for a, b in zip(items[::2], items[1::2])]
        items = paired + items[len(items) - len(items) % 2:]
    return items[0]


def chain_kernel(space, tm, times, steps, anomalies_ref, index_ref, weight_ref, out_ref,
                 cells, index, weight, gram, near, joint, far, partner, matrix, weights, products, chains_ref,
                 load_sem, index_sem, weight_sem,
                 near_send, near_recv, far_send, far_recv, partner_send, partner_recv, share_send, share_recv,
                 spread_send, spread_recv, pass_send, pass_recv, time_send, time_recv,
                 relay_send, relay_recv):
    members = matrix.shape[0]
    me = lax.axis_index("space")
    mine = lax.axis_index("tm")
    rows = times * members // space
    team = space // times
    owned = me // team
    place = me % team
    base = owned * team

    def row_slice(number):
        return pl.ds(pl.multiple_of(number * rows, rows), rows)

    def to(source, target, send, recv, **device):
        return pltpu.make_async_remote_copy(
            src_ref=source, dst_ref=target, send_sem=send, recv_sem=recv,
            device_id=device, device_id_type=MESH,
        )

    order = [(owned + 1 + i) % times for i in range(times)]
    index_load = pltpu.make_async_copy(index_ref, index, index_sem)
    weight_load = pltpu.make_async_copy(weight_ref, weight, weight_sem)
    loads = [
        pltpu.make_async_copy(anomalies_ref.at[slot], cells.at[i], load_sem.at[i])
        for i, slot in enumerate(order)
    ]
    index_load.start()
    loads[0].start()
    weight_load.start()
    for load in loads[1:]:
        load.start()

    barrier = pltpu.get_barrier_semaphore()
    for d in range(1, space):
        pl.semaphore_signal(barrier, inc=1, device_id={"space": (me + d) % space}, device_id_type=MESH)
    for d in range(1, tm):
        pl.semaphore_signal(barrier, inc=1, device_id={"tm": (mine + d) % tm}, device_id_type=MESH)
    index_load.wait()
    weight_load.wait()

    sends = []
    near_copies = []
    far_copies = []

    def pass_on(i):
        piece = gram[order[i], row_slice(place), :]
        for copy in near_copies[i]:
            copy.wait_recv()
        for e in range(1, team):
            piece = piece + near[i, e]
        joint[i] = piece
        copy = to(joint.at[i], far.at[i], far_send.at[i], far_recv.at[i],
                  space=order[i] * team + place)
        copy.start()
        far_copies.append(copy)

    roots = [
        cell_roots(index[pl.ds(slot, 1), :], weight[pl.ds(slot, 1), :], cells.shape[2])
        for slot in order
    ]
    for i, slot in enumerate(order):
        loads[i].wait()
        gram[slot] = gram_of(cells.at[i], roots[i])
        if i == 0:
            pl.semaphore_wait(barrier, space + tm - 2)
        if i < times - 1:
            near_copies.append([])
            for e in range(1, team):
                peer = (place + e) % team
                copy = to(gram.at[slot, row_slice(peer)], near.at[i, e], near_send.at[i, e],
                          near_recv.at[i, e], space=base + peer)
                copy.start()
                near_copies[i].append(copy)
        if 2 <= i < times - 1:
            pass_on(i - 2)
    partners = []
    for e in range(1, team):
        copy = to(gram.at[owned], partner.at[e], partner_send.at[e], partner_recv.at[e],
                  space=base + (place + e) % team)
        copy.start()
        partners.append(copy)
    for i in range(max(times - 3, 0), times - 1):
        pass_on(i)
    for copy in far_copies:
        copy.wait_recv()
    matrix[row_slice(place), :] = jnp.sum(far[...], axis=0)
    shares = []
    for e in range(1, team):
        copy = to(matrix.at[row_slice(place)], matrix.at[row_slice(place)], share_send.at[e],
                  share_recv.at[e], space=base + (place + e) % team)
        copy.start()
        shares.append(copy)
    total = gram[owned]
    for copy in partners:
        copy.wait_recv()
    for e in range(1, team):
        total = total + partner[e]
    for e in range(1, team):
        origin = (place + team - e) % team
        to(matrix.at[row_slice(origin)], matrix.at[row_slice(origin)], share_send.at[e],
           share_recv.at[e], space=base + origin).wait_recv()
    total = total + matrix[...]

    identity = (
        lax.broadcasted_iota(jnp.int32, (members, members), 0)
        == lax.broadcasted_iota(jnp.int32, (members, members), 1)
    ).astype(jnp.float32)
    spread = float(members - 1)
    weights[owned] = inverse_of(identity + total / spread, identity, steps)

    def own_rows(slot):
        return weights.at[slot, row_slice(place)]

    for d in sorted(range(1, times), key=lambda d: abs(2 * d - times)):
        copy = to(own_rows(owned), own_rows(owned), spread_send.at[d], spread_recv.at[d],
                  space=((owned + d) % times) * team + place)
        copy.start()
        sends.append(copy)
    for d in range(1, times):
        slot = (owned + times - d) % times
        to(own_rows(slot), own_rows(slot), spread_send.at[d], spread_recv.at[d],
           space=slot * team + place).wait_recv()
        for e in range(1, team):
            copy = to(own_rows(slot), own_rows(slot), pass_send.at[d, e], pass_recv.at[d, e],
                      space=base + (place + e) % team)
            copy.start()
            sends.append(copy)
    for d in range(1, times):
        slot = (owned + times - d) % times
        for e in range(1, team):
            origin = (place + team - e) % team
            there = weights.at[slot, row_slice(origin)]
            to(there, there, pass_send.at[d, e], pass_recv.at[d, e], space=base + origin).wait_recv()

    each = [weights[t] for t in range(times)]

    @pl.when(mine > 0)
    def _():
        products[mine] = tree(each)

    def product_rows(slot, number):
        return products.at[slot, row_slice(number)]

    for d in range(tm - 1, 0, -1):
        @pl.when(mine >= d)
        def _(d=d):
            to(product_rows(mine, place), product_rows(mine, place), time_send.at[d],
               time_recv.at[d], tm=jnp.maximum(mine - d, 0)).start()

    tails = [identity]
    for t in range(times - 1, 0, -1):
        tails.append(near_dot(each[t], tails[-1]) if t < times - 1 else each[t])
    tails = tails[::-1]

    for d in range(1, tm):
        @pl.when(mine + d < tm)
        def _(d=d):
            slot = jnp.minimum(mine + d, tm - 1)
            to(product_rows(slot, place), product_rows(slot, place), time_send.at[d],
               time_recv.at[d], tm=slot).wait_recv()
            for e in range(1, team):
                to(product_rows(slot, place), product_rows(slot, place), relay_send.at[d, e],
                   relay_recv.at[d, e], space=base + (place + e) % team).start()
    chains_ref[...] = jnp.concatenate(tails, axis=0)
    for d in range(1, tm):
        @pl.when(mine + d < tm)
        def _(d=d):
            slot = jnp.minimum(mine + d, tm - 1)
            for e in range(1, team):
                origin = (place + team - e) % team
                to(product_rows(slot, origin), product_rows(slot, origin), relay_send.at[d, e],
                   relay_recv.at[d, e], space=base + origin).wait_recv()
            chains_ref[...] = near_dot(chains_ref[...], products[slot])

    for t in range(times):
        out_ref[t] = chains_ref[t * members:(t + 1) * members].T.astype(out_ref.dtype)

    for copy in sum(near_copies, sends + shares + partners + far_copies):
        copy.wait_send()
    for d in range(1, tm):
        @pl.when(mine >= d)
        def _(d=d):
            to(product_rows(mine, place), product_rows(mine, place), time_send.at[d],
               time_recv.at[d], tm=jnp.maximum(mine - d, 0)).wait_send()

        @pl.when(mine + d < tm)
        def _(d=d):
            slot = jnp.minimum(mine + d, tm - 1)
            for e in range(1, team):
                to(product_rows(slot, place), product_rows(slot, place), relay_send.at[d, e],
                   relay_recv.at[d, e], space=base + (place + e) % team).wait_send()


def smooth_kernel(chain_ref, anomalies_ref, out_ref, done, done_sem):
    times, members, cells = anomalies_ref.shape
    parts = done_sem.shape[1]
    width = cells // parts
    copies = []
    for t in range(times):
        for c in range(parts):
            part = slice(c * width, (c + 1) * width)
            done[t, :, part] = jnp.dot(
                chain_ref[t], anomalies_ref[t, :, part], preferred_element_type=jnp.float32
            ).astype(done.dtype)
            copy = pltpu.make_async_copy(
                done.at[t, :, part], out_ref.at[t, :, part], done_sem.at[t, c]
            )
            copy.start()
            copies.append(copy)
    for copy in copies:
        copy.wait()


def per_device(space, tm, anomalies, obs_index, obs_weight):
    times, members, cells = anomalies.shape
    obs = obs_index.shape[1]
    whole_vmem = pl.BlockSpec(memory_space=pltpu.VMEM)

    bound = 1.0 + members * obs * space * LARGEST_SCALED**2 / (members - 1)
    steps = math.ceil(math.log(bound / 4.0, 4)) + 3
    rows = times * members // space
    team = space // times
    dma = pltpu.SemaphoreType.DMA
    in_hbm = pl.BlockSpec(memory_space=pltpu.HBM)
    wide = jnp.float32
    square_wide = (members, members)
    chains = pl.pallas_call(
        functools.partial(chain_kernel, space, tm, times, steps),
        in_specs=[in_hbm] * 3,
        out_specs=whole_vmem,
        out_shape=jax.ShapeDtypeStruct((times, members, members), jnp.bfloat16),
        scratch_shapes=[
            pltpu.VMEM(anomalies.shape, anomalies.dtype),
            pltpu.VMEM(obs_index.shape, obs_index.dtype),
            pltpu.VMEM(obs_weight.shape, obs_weight.dtype),
            pltpu.VMEM((times, *square_wide), wide),
            pltpu.VMEM((times - 1, team, rows, members), wide),
            pltpu.VMEM((times - 1, rows, members), wide),
            pltpu.VMEM((times - 1, rows, members), wide),
            pltpu.VMEM((team, *square_wide), wide),
            pltpu.VMEM(square_wide, wide),
            pltpu.VMEM((times, *square_wide), wide),
            pltpu.VMEM((tm, *square_wide), wide),
            pltpu.VMEM((times * members, members), wide),
            dma((times,)), dma, dma,
            dma((times, team)), dma((times, team)), dma((times,)), dma((times,)), dma((team,)), dma((team,)),
            dma((team,)), dma((team,)), dma((times,)), dma((times,)),
            dma((times, team)), dma((times, team)), dma((tm,)), dma((tm,)),
            dma((tm, team)), dma((tm, team)),
        ],
        compiler_params=pltpu.CompilerParams(
            collective_id=0, has_side_effects=True, vmem_limit_bytes=40 * 2**20
        ),
    )(*(pltpu.with_memory_space_constraint(x, pltpu.HBM) for x in (anomalies, obs_index, obs_weight)))

    return pl.pallas_call(
        smooth_kernel,
        in_specs=[whole_vmem, whole_vmem],
        out_specs=in_hbm,
        out_shape=jax.ShapeDtypeStruct(anomalies.shape, anomalies.dtype),
        scratch_shapes=[pltpu.VMEM(anomalies.shape, anomalies.dtype), dma((times, 2))],
        compiler_params=pltpu.CompilerParams(vmem_limit_bytes=40 * 2**20),
    )(chains, anomalies)


def solution(mesh):
    return jax.shard_map(
        functools.partial(per_device, mesh.shape["space"], mesh.shape["tm"]),
        mesh=mesh,
        in_specs=(P("tm", None, "space"), P("tm", "space"), P("tm", "space")),
        out_specs=P("tm", None, "space"),
        check_vma=False,
    )
```
